128 devices in a mesh: shard: 32 (over y, z, core), grp: 4 (over x).
Axes of the slice: x: 4, y: 4, z: 4, core: 2. Of those that a mesh axis runs over, the one named last changes fastest.
Arguments:
- corpus: float32 [8192, 8, 768], P(('shard', 'grp')), may hold values from -6 to 6
- block_rows: int32 [8192], P(('shard', 'grp')), may hold values from 1 to 8
- targets: int32 [8192, 1], P(('shard', 'grp')), may hold values from 0 to 31; in each aligned block of 64 rows (0 to 63, 64 to 127, ...) at most 4 rows name the same one
- assign: int32 [8192, 8], P(('shard', 'grp')), may hold values from 0 to 4095
- codes: int32 [8192, 8, 96], P(('shard', 'grp')), may hold values from 0 to 255
- centroids: float32 [4096, 768], P('shard'), may hold values from -4 to 4
- codebook: float32 [256, 768], replicated, may hold values from -4 to 4
Outputs:
- new_centroids: float32 [4096, 768], P('shard')
- moved_error: bfloat16 [16384, 8, 768], P(('shard', 'grp'))
- new_codebook: float32 [256, 768], replicated
The draws below stay inside these ranges and needn't reach their ends.
Inputs may be any that keep to these rules, and one draw needn't show every extreme that they name: `targets`: among the 64 blocks of one device no shard is named more than 4 times, and some device names one shard exactly 4 times.
All inputs are finite; a program needn't handle non-finite values.
Results may differ from the reference program's by a relative error of at most 0.001.
Values sent between devices are 32-bit elements; how exact they have to be, the bound alone decides.
No kernel may reach another device: no remote copies, remote signals or barrier semaphores. Data moves between devices by JAX's collectives and lax.ppermute only.
A program may use at most 192 MiB of HBM per device.

```python
import math
import jax
import jax.numpy as jnp
import numpy as np

D = 768
M = 96
SUB = 8
CODES = 256
K = 4096
BLK = 8
BLK_DEV = 64
CAP = 4
SLOTS_DEV = 128
SLOTS = 16384
BLOCKS = 8192
N_SHARD = 32
N_GRP = 4


def set_ends(result, rng, low, largest):
    longest = result.shape.index(max(result.shape))
    spots = []
    for shift in (0, 1):
        where = [jax.random.randint(jax.random.fold_in(rng, axis), (), 0, length) for axis, length in enumerate(result.shape)]
        where[longest] = (where[longest] + shift) % result.shape[longest]
        spots.append(tuple(where))
    return result.at[spots[0]].set(low).at[spots[1]].set(largest)


def shard_levels(stream_key, extent, split, least, top_value):
    level = 1.0
    for axis_at, shards_of in split:
        steps = jax.random.uniform(jax.random.fold_in(jax.random.fold_in(stream_key, 6), axis_at), (shards_of,), jnp.float32, least / len(split), top_value / len(split))
        level = level * jnp.repeat(jnp.exp(steps), extent[axis_at] // shards_of).reshape((-1,) + (1,) * (len(extent) - 1 - axis_at))
    return level


def rank_bounds(number_of, slope):
    portions = [(1 << 20) // math.isqrt(rank ** slope) + 1 for rank in range(1, number_of + 1)]
    width = 1 + sum(portions) // (1 << 30)
    return np.cumsum(np.array([max(1, weight // width) for weight in portions]))


def ranked_ids(own_key, extent, count, lean):
    listing = rank_bounds(count, lean)
    ticket = jax.random.randint(jax.random.fold_in(own_key, 1), extent, 0, int(listing[count - 1]))
    standing = jnp.searchsorted(jnp.asarray(listing, jnp.int32), ticket, side="right")
    return jax.random.permutation(jax.random.fold_in(own_key, 2), count)[standing].astype(jnp.int32)


def shared_out(rng, own, number, rows, number_of, top, limit, lean):
    ranking = jax.random.permutation(rng, number_of)
    crowded, common = portions_of(number_of, rows * top, limit, lean, True), portions_of(number_of, rows * top, limit, lean, False)
    places = jnp.arange(number_of)

    def named(sizes, rotation):
        used = int((sizes > 0).sum())
        fixed = max(1, used // 4)
        shifted = fixed + (places - fixed + rotation * (used - fixed)) % max(1, number_of - fixed)
        return jnp.zeros((number_of,), jnp.int32).at[ranking[jnp.where(places < fixed, places, shifted)]].set(jnp.asarray(sizes, jnp.int32))

    sizes = jnp.where(number % 4 == 0, named(crowded, number // 4), named(common, number - number // 4 - 1))
    mixed = jax.random.permutation(jax.random.fold_in(own, 3), number_of)
    giver, taker = mixed[0:number_of // 2 * 2:2], mixed[1:number_of // 2 * 2:2]
    margin = jnp.minimum(sizes[giver] - 1, limit - sizes[taker]) // 2
    margin = jnp.where((giver == ranking[0]) | (taker == ranking[0]) | (sizes[taker] == 0), 0, jnp.maximum(margin, 0))
    shifted = jax.random.randint(jax.random.fold_in(own, 4), (number_of // 2,), 0, 1 << 20) % (margin + 1)
    sizes = sizes.at[giver].add(-shifted).at[taker].add(shifted)
    labels = jnp.searchsorted(jnp.cumsum(sizes), jnp.arange(rows * top), side="right").astype(jnp.int32)
    table = labels.reshape(top, rows).T
    table = table[jax.random.permutation(jax.random.fold_in(own, 1), rows)]
    rotation = jax.random.randint(jax.random.fold_in(own, 2), (rows, 1), 0, top)
    return jnp.take_along_axis(table, (jnp.arange(top)[None, :] + rotation) % top, axis=1)


def portions_of(amount, total, bound, slope, full):
    portions = [(1 << 20) // math.isqrt(grade ** slope) + 1 for grade in range(1, amount + 1)]
    largest = bound if full else min(bound, max(-(-total // amount), total * portions[0] // sum(portions)))
    least = 1 if total - largest >= amount - 1 else 0
    given, rest = [largest] + [least] * (amount - 1), total - largest - least * (amount - 1)
    while rest > 0:
        candidates = [i for i in range(1, amount) if given[i] < largest] or [i for i in range(1, amount) if given[i] < bound]
        whole, budget = sum([portions[i] for i in candidates]), rest
        for i in candidates:
            more = min(bound - given[i], max(1, budget * portions[i] // whole), rest)
            given[i] = given[i] + more
            rest = rest - more
    return np.array(given)


def centred(own_key, extent, spread, bound, split=(), held_as=jnp.bfloat16):
    values = spread * jax.random.normal(own_key, extent, jnp.float32)
    if split:
        values = values * shard_levels(own_key, extent, split, -0.22, 0.18)
    return jnp.clip(values, -bound, bound).astype(held_as)


def setup_inputs(seed: int = 0) -> dict:
    key_list = jax.random.split(jax.random.key(seed), 8)
    corpus = centred(key_list[0], (BLOCKS, BLK, D), 1.0, 6.0, ((0, 128),), jnp.float32)
    block_rows = set_ends(jax.random.randint(key_list[1], (BLOCKS,), 1, BLK + 1), jax.random.fold_in(key_list[1], 1), 1, BLK).astype(jnp.int32)
    targets_keys = jax.random.split(jax.random.fold_in(key_list[2], 1), BLOCKS // BLK_DEV)
    targets_turns = jax.random.permutation(jax.random.fold_in(key_list[2], 3), BLOCKS // BLK_DEV)
    targets = jax.vmap(lambda own, number: shared_out(jax.random.fold_in(key_list[2], 2), own, number, BLK_DEV, N_SHARD, 1, CAP, 2))(targets_keys, targets_turns).reshape((BLOCKS, 1))
    assign = set_ends(ranked_ids(key_list[3], (BLOCKS, BLK), K, 1), jax.random.fold_in(key_list[3], 3), 0, K - 1).astype(jnp.int32)
    codes = set_ends(ranked_ids(key_list[4], (BLOCKS, BLK, M), CODES, 2), jax.random.fold_in(key_list[4], 3), 0, CODES - 1).astype(jnp.int32)
    centroids = centred(key_list[5], (K, D), 0.5, 4.0, ((0, 32),), jnp.float32)
    codebook = centred(key_list[6], (CODES, D), 0.5, 4.0, (), jnp.float32)
    return dict(corpus=corpus, block_rows=block_rows, targets=targets, assign=assign, codes=codes, centroids=centroids, codebook=codebook)


prior_weight = 8.0


def reference(corpus, block_rows, targets, assign, codes, centroids, codebook):
    blocks = corpus.shape[0]
    devs = blocks // BLK_DEV
    weight = (jnp.arange(BLK, dtype=jnp.int32)[None, :] < block_rows[:, None]).astype(jnp.float32)
    flat_weight = weight.reshape(-1)
    ids = assign.reshape(-1)
    sums = jax.ops.segment_sum(corpus.reshape(-1, D) * flat_weight[:, None], ids, num_segments=K)
    counts = jax.ops.segment_sum(flat_weight, ids, num_segments=K)
    new_centroids = (sums + prior_weight * centroids) / (counts[:, None] + prior_weight)
    resid = corpus - jnp.take(new_centroids, assign, axis=0)
    pieces = (flat_weight[:, None, None] * resid.reshape(-1, M, SUB)).reshape(-1, SUB)
    code_ids = (codes.reshape(-1, M) + CODES * jnp.arange(M, dtype=jnp.int32)[None, :]).reshape(-1)
    csum = jax.ops.segment_sum(pieces, code_ids, num_segments=M * CODES)
    spread_weight = jnp.broadcast_to(flat_weight[:, None], (flat_weight.shape[0], M)).reshape(-1)
    ccount = jax.ops.segment_sum(spread_weight, code_ids, num_segments=M * CODES)
    old_book = codebook.reshape(CODES, M, SUB).transpose(1, 0, 2)
    fresh_book = (csum.reshape(M, CODES, SUB) + prior_weight * old_book) / (ccount.reshape(M, CODES, 1) + prior_weight)
    words = fresh_book[jnp.arange(M, dtype=jnp.int32)[None, None, :], codes]
    err = ((resid - words.reshape(blocks, BLK, D)) * weight[:, :, None]).astype(jnp.bfloat16)
    dest = targets[:, 0].reshape(devs, BLK_DEV)
    order = jnp.arange(BLK_DEV, dtype=jnp.int32)
    same = (dest[:, :, None] == dest[:, None, :]) & (order[None, None, :] < order[None, :, None])
    rank = jnp.sum(same.astype(jnp.int32), axis=2)
    device = jnp.arange(devs, dtype=jnp.int32)[:, None]
    slot = ((dest * N_GRP + device % N_GRP) * SLOTS_DEV + (device // N_GRP) * CAP + rank).reshape(-1)
    moved_error = jnp.zeros((SLOTS, BLK, D), jnp.bfloat16).at[slot].set(err)
    new_codebook = fresh_book.transpose(1, 0, 2).reshape(CODES, D)
    return new_centroids, moved_error, new_codebook
```

```python
import jax
import jax.numpy as jnp
from jax import lax
from jax.experimental import pallas as pl
from jax.experimental.pallas import tpu as pltpu
from jax.sharding import PartitionSpec as P

PRIOR = 8.0
BOTH = ("shard", "grp")
F32 = jnp.float32
BF16 = jnp.bfloat16
VMEM_LIMIT = 56 * 1024 * 1024

CH = 40
FIRST = (0, 0, 1, 2)
SECOND = (0, 1, 2, 2)


def call(body, out, scratch=(), flops=0, moved=0):
    return pl.pallas_call(
        body,
        out_shape=out,
        scratch_shapes=list(scratch),
        compiler_params=pltpu.CompilerParams(vmem_limit_bytes=VMEM_LIMIT),
        cost_estimate=pl.CostEstimate(flops=flops, bytes_accessed=moved, transcendentals=0),
    )


def nt(a, b):
    return lax.dot_general(a, b, (((1,), (1,)), ((), ())), preferred_element_type=F32)


def nn(a, b):
    return lax.dot_general(a, b, (((1,), (0,)), ((), ())), preferred_element_type=F32)


def lanes(shape):
    return lax.broadcasted_iota(jnp.int32, shape, len(shape) - 1)


def subs(shape):
    return lax.broadcasted_iota(jnp.int32, shape, len(shape) - 2)


def split(x):
    hi = x.astype(BF16).astype(F32)
    return hi, x - hi


def send_body(corpus, codes, meta, cent, out, turned, words, rows_s):
    for p in range(4):
        for w in range(6):
            for h in range(2):
                rows_s[h * 64 : (h + 1) * 64, :] = corpus[w, pl.ds(2 * p + h, 64, stride=8), :]
            turned[w * 128 : (w + 1) * 128, :] = rows_s[...].T
        for c in range(6):
            out[pl.ds(p * 8 + c, 128, stride=CH), :] = turned[pl.ds(c, 128, stride=6), :]
        for h in range(2):
            rows_s[h * 64 : (h + 1) * 64, :] = codes[pl.ds(2 * p + h, 64, stride=8), :]
        words[...] = rows_s[...].T
        for j in range(4):
            for k, pick in ((6, FIRST[j]), (7, SECOND[j])):
                out[pl.ds(j * CH + p * 8 + k, 32, stride=4 * CH), :] = words[pl.ds(pick, 32, stride=3), :]
    for k in range(5):
        out[pl.ds(32 + k, 128, stride=CH), :] = jnp.broadcast_to(meta[k : k + 1, :], (128, 128))
    for w in range(6):
        rows_s[...] = jnp.zeros((128, 128), F32)
        rows_s[0:32, :] = cent[:, w * 128 : (w + 1) * 128]
        turned[w * 128 : (w + 1) * 128, :] = rows_s[...].T
    parts = [turned[pl.ds(c, 128, stride=6), :] for c in range(6)]
    for k, cols in ((5, (0, 1, 2, 3)), (6, (4, 5))):
        row = parts[cols[0]]
        for i, c in enumerate(cols[1:], 1):
            row = row + pltpu.roll(parts[c], 32 * i, 1)
        out[pl.ds(32 + k, 128, stride=CH), :] = row
    out[pl.ds(39, 128, stride=CH), :] = jnp.zeros((128, 128), F32)


def row_info(tile):
    lane = lanes((8, 128))
    counts = tile[4:5, :]
    counts = jnp.where(lane[0:1] < 64, pltpu.roll(counts, 64, 1), counts)
    place = 2 * subs((8, 128)) + (lane >= 64).astype(jnp.int32)
    used = place < counts.astype(jnp.int32)
    return tile.astype(jnp.int32), used


GRP_SRC = 4


def sums_body(recv, out, acc):
    acc[...] = jnp.zeros((256, 256), F32)
    sub8 = subs((8, 128))
    digits = subs((256, 128)).astype(F32).astype(BF16)

    def step(i, carry):
        left, right = [], []
        for k in range(GRP_SRC):
            base = pl.multiple_of((i * GRP_SRC + k) * CH, 8)
            label, used = row_info(recv[pl.ds(base + 32, 8), :])
            low = jnp.where(used, label & 255, -1).astype(F32).astype(BF16)
            high = (label >> 8).astype(F32).astype(BF16)
            for p in range(4):
                x = recv[pl.ds(base + 8 * p, 8), :]
                hi, lo = split(x)
                hi = jnp.where(sub8 < 6, hi, jnp.where(sub8 == 6, 1.0, 0.0))
                lo = jnp.where(sub8 < 6, lo, 0.0)
                xb = jnp.concatenate([hi, lo], 0).astype(BF16)
                sel = jnp.broadcast_to(high[p : p + 1, :], (16, 128))
                left.append(
                    jnp.concatenate([jnp.where(sel == jnp.asarray(v, BF16), xb, jnp.zeros_like(xb)) for v in range(16)], 0)
                )
                right.append(jnp.where(digits == jnp.broadcast_to(low[p : p + 1, :], (256, 128)),
                                       jnp.ones((256, 128), BF16), jnp.zeros((256, 128), BF16)))
        acc[...] += nt(jnp.concatenate(left, 1), jnp.concatenate(right, 1))
        return carry

    lax.fori_loop(0, 128 // GRP_SRC, step, 0)

    lane = lanes((8, 128))

    def finish(s, carry):
        sel = s // 2
        old = jnp.zeros((8, 128), F32)
        for g in range(4):
            tile = recv[pl.ds(pl.multiple_of((s * 4 + g) * CH + 32, 8), 8), :]
            both = jnp.where(sub8 < 4, jnp.broadcast_to(tile[5:6, :], (8, 128)), jnp.broadcast_to(tile[6:7, :], (8, 128)))
            moved = jnp.zeros((8, 128), F32)
            for c in range(4):
                moved = jnp.where((sub8 & 3) == c, pltpu.roll(both, (32 * (g - c)) % 128, 1), moved)
            old = jnp.where((lane >> 5) == g, moved, old)
        old = jnp.where(sub8 < 6, old, 0.0)
        rows = acc[pl.ds(pl.multiple_of(sel * 16, 16), 16), :]
        rows = jnp.where((s & 1) == 0, rows[:, :128], rows[:, 128:])
        total = rows[0:8] + rows[8:16]
        count = jnp.broadcast_to(total[6:7, :], (8, 128))
        fresh = (total + PRIOR * old) / (count + PRIOR)
        out[s] = jnp.where(sub8 < 6, fresh, 0.0)
        return carry

    lax.fori_loop(0, 32, finish, 0)


def code_digits(x, first, second_cols, used):
    a = jnp.broadcast_to(x[6:7, :], (8, 128))
    b = jnp.broadcast_to(x[7:8, :], (8, 128))
    return a, b


def resid_body(place, recv, fresh, book, resid, table, shown, left, acc):
    first = place[0]
    sub8 = subs((8, 128))
    lane = lanes((8, 128))
    digits = subs((256, 128)).astype(F32).astype(BF16)
    digit64 = subs((64, 128)).astype(F32).astype(BF16)
    for sel in range(16):
        for h in range(2):
            hi, lo = split(fresh[2 * sel + h])
            left[sel * 16 : (sel + 1) * 16, h * 128 : (h + 1) * 128] = jnp.concatenate([hi, lo], 0).astype(BF16)
    acc[...] = jnp.zeros((64, 128), F32)
    one, zero = jnp.ones((), BF16), jnp.zeros((), BF16)
    is_first = (sub8 < first) | (sub8 == 6)

    def step(i, carry):
        lhs, rhs = [], []
        for k in range(2):
            src = i * 2 + k
            base = pl.multiple_of(src * CH, 8)
            label, used = row_info(recv[pl.ds(base + 32, 8), :])
            low = (label & 255).astype(F32).astype(BF16)
            high = label >> 8
            hot = [jnp.where(digits == jnp.broadcast_to(low[p : p + 1, :], (256, 128)),
                             jnp.ones((256, 128), BF16), jnp.zeros((256, 128), BF16)) for p in range(4)]
            got = nn(left[...], jnp.concatenate(hot, 1))
            for p in range(4):
                x = recv[pl.ds(base + 8 * p, 8), :]
                sel = jnp.broadcast_to(high[p : p + 1, :], (8, 128))
                ghi = jnp.zeros((8, 128), F32)
                glo = jnp.zeros((8, 128), F32)
                for v in range(16):
                    hit = sel == v
                    ghi = jnp.where(hit, got[v * 16 : v * 16 + 8, p * 128 : (p + 1) * 128], ghi)
                    glo = jnp.where(hit, got[v * 16 + 8 : v * 16 + 16, p * 128 : (p + 1) * 128], glo)
                r = x - (ghi + glo)
                resid[src * 4 + p] = r
                a = jnp.broadcast_to(x[6:7, :], (8, 128))
                b = jnp.broadcast_to(x[7:8, :], (8, 128))
                code = jnp.where(is_first, a, b).astype(jnp.int32)
                use = used[p : p + 1, :]
                pick = jnp.where(jnp.broadcast_to(use, (8, 128)), code >> 6, -1).astype(F32)
                pick = jnp.concatenate([pick, pick], 0).astype(BF16)
                hi, lo = split(r)
                hi = jnp.where(sub8 < 6, hi, 1.0)
                lo = jnp.where(sub8 < 6, lo, 0.0)
                rb = jnp.concatenate([hi, lo], 0).astype(BF16)
                lhs.append(jnp.concatenate([jnp.where(pick == jnp.asarray(v, BF16), rb, jnp.zeros_like(rb)) for v in range(4)], 0))
                da = (x[6:7, :].astype(jnp.int32) & 63).astype(F32).astype(BF16)
                db = (x[7:8, :].astype(jnp.int32) & 63).astype(F32).astype(BF16)
                rhs.append(jnp.concatenate(
                    [jnp.where(digit64 == jnp.broadcast_to(d, (64, 128)), jnp.ones((64, 128), BF16), jnp.zeros((64, 128), BF16))
                     for d in (da, db)], 0))
        acc[...] += nt(jnp.concatenate(lhs, 1), jnp.concatenate(rhs, 1))
        return carry

    lax.fori_loop(0, 64, step, 0)

    valid = ((sub8 < first) == (lane < 64)) & (sub8 < 6)
    made = []
    for sel in range(4):
        total = acc[sel * 16 : sel * 16 + 8, :] + acc[sel * 16 + 8 : sel * 16 + 16, :]
        count = jnp.where(lane < 64, jnp.broadcast_to(total[6:7, :], (8, 128)), jnp.broadcast_to(total[7:8, :], (8, 128)))
        new = (total + PRIOR * book[sel]) / (count + PRIOR)
        new = jnp.where(valid, new, 0.0)
        table[sel] = new
        made.append(new + pltpu.roll(new, 64, 1))
    shown[0] = jnp.where(lane < 64, made[0], made[1])
    shown[1] = jnp.where(lane < 64, made[2], made[3])


def error_body(place, recv, resid, table, out, err, mixed, left):
    first = place[0]
    sub8 = subs((8, 128))
    lane = lanes((8, 128))
    digit64 = subs((64, 128)).astype(F32).astype(BF16)
    is_first = sub8 < first
    for sel in range(4):
        hi, lo = split(table[sel])
        left[sel * 16 : (sel + 1) * 16, :] = jnp.concatenate([hi, lo], 0).astype(BF16)

    def look(src, carry):
        base = pl.multiple_of(src * CH, 8)
        unused, used = row_info(recv[pl.ds(base + 32, 8), :])
        hot = []
        for p in range(4):
            r = resid[src * 4 + p]
            da = (r[6:7, :].astype(jnp.int32) & 63).astype(F32).astype(BF16)
            db = (r[7:8, :].astype(jnp.int32) & 63).astype(F32).astype(BF16)
            hot.append(jnp.concatenate(
                [jnp.where(digit64 == jnp.broadcast_to(d, (64, 128)), jnp.ones((64, 128), BF16), jnp.zeros((64, 128), BF16))
                 for d in (da, db)], 0))
        got = nn(left[...], jnp.concatenate(hot, 1))
        for p in range(4):
            r = resid[src * 4 + p]
            a = jnp.broadcast_to(r[6:7, :], (8, 128))
            b = jnp.broadcast_to(r[7:8, :], (8, 128))
            pick = jnp.where(is_first, a, b).astype(jnp.int32) >> 6
            whi = jnp.zeros((8, 128), F32)
            wlo = jnp.zeros((8, 128), F32)
            for v in range(4):
                hit = pick == v
                whi = jnp.where(hit, got[v * 16 : v * 16 + 8, p * 128 : (p + 1) * 128], whi)
                wlo = jnp.where(hit, got[v * 16 + 8 : v * 16 + 16, p * 128 : (p + 1) * 128], wlo)
            e = jnp.where(jnp.broadcast_to(used[p : p + 1, :], (8, 128)) & (sub8 < 6), r - (whi + wlo), 0.0)
            err[src * 4 + p] = e
        return carry

    lax.fori_loop(0, 128, look, 0)

    spots = subs((512, 128))
    spot_lane = lanes((1, 128))

    def group(g, carry):
        def gather(sh, carry2):
            cols, hots = [], []
            for pair in range(2):
                srcs = [sh * 16 + (2 * pair + q) * 4 + g for q in range(2)]
                aims = []
                for q in range(2):
                    row = recv[pl.ds(srcs[q] * CH + 36, 1), :].astype(jnp.int32)
                    aims.append((row >> 2) * 16 + (row & 3) + (2 * pair + q) * 4)
                aim = jnp.where(spot_lane < 64, aims[0], pltpu.roll(aims[1], 64, 1))
                hots.append(jnp.where(spots == jnp.broadcast_to(aim, (512, 128)), 1.0, 0.0).astype(BF16))
                rows = []
                for p in range(4):
                    e0 = err[srcs[0] * 4 + p]
                    e1 = err[srcs[1] * 4 + p]
                    rows.append(jnp.where(lane < 64, e0, pltpu.roll(e1, 64, 1)))
                    rows.append(jnp.where(lane < 64, pltpu.roll(e0, 64, 1), e1))
                cols.append(jnp.concatenate(rows, 0).astype(BF16))
            mixed[sh] = nt(jnp.concatenate(cols, 1), jnp.concatenate(hots, 1))
            return carry2

        lax.fori_loop(0, 8, gather, 0)
        for v in range(4):
            for r in range(8):
                z = [mixed[sh, r * 8 : (r + 1) * 8, v * 128 : (v + 1) * 128] for sh in range(8)]
                for bit in range(3):
                    step = 1 << bit
                    keep = ((lane >> (4 + bit)) & 1) == 0
                    nz = list(z)
                    for i in range(8):
                        if i & step:
                            continue
                        a, b = z[i], z[i | step]
                        nz[i] = jnp.where(keep, a, pltpu.roll(b, 16 * step, 1))
                        nz[i | step] = jnp.where(keep, pltpu.roll(a, 128 - 16 * step, 1), b)
                    z = nz
                for tl in range(8):
                    t = 8 * v + tl
                    out[pl.ds((t * 4 + g) * 48 + r, 6, stride=8), :] = z[tl][0:6, :]
        return carry

    lax.fori_loop(0, 4, group, 0)


def place_body(recv, out, turned):
    for r in range(8):
        for w in range(6):
            turned[w, pl.ds(r, 128, stride=8), :] = recv[pl.ds(w * 1024 + r, 128, stride=8), :].T
    for w in range(6):
        out[:, :, w * 128 : (w + 1) * 128] = turned[w].reshape(128, 8, 128).astype(BF16)


def columns_body(parts, recv, out, turned):
    for h in range(parts):
        for c in range(6):
            turned[pl.ds(c, 128, stride=6), :] = recv[pl.ds(h * 8 + c, 128, stride=8 * parts), :]
        for w in range(6):
            out[h * 128 : (h + 1) * 128, w * 128 : (w + 1) * 128] = turned[w * 128 : (w + 1) * 128, :].T


def slot_ranks(dest):
    count = dest.shape[0]
    order = jnp.arange(count, dtype=jnp.int32)
    same = (dest[:, None] == dest[None, :]) & (order[None, :] < order[:, None])
    return jnp.sum(same.astype(jnp.int32), axis=1)


def local(corpus, block_rows, targets, assign, codes, centroids, codebook):
    grp = lax.axis_index("grp")
    me = lax.axis_index("shard") * 4 + grp
    first = jnp.where(grp == 1, 2, jnp.where(grp == 2, 4, 6)).astype(jnp.int32).reshape(1)
    dest = targets[:, 0]
    slot = dest * 4 + slot_ranks(dest)
    meta = jnp.concatenate(
        [assign.T.reshape(4, 128), jnp.concatenate([slot, block_rows]).reshape(1, 128), jnp.zeros((3, 128), jnp.int32)], 0
    ).astype(F32)
    quarter = lax.dynamic_slice(centroids, (grp * 32, 0), (32, 768))
    rows = corpus.reshape(512, 6, 128).transpose(1, 0, 2)
    words = jnp.pad(codes.reshape(512, 96).astype(F32), ((0, 0), (0, 32)))

    sent = call(
        send_body,
        jax.ShapeDtypeStruct((128 * CH, 128), F32),
        [pltpu.VMEM((768, 128), F32), pltpu.VMEM((128, 128), F32), pltpu.VMEM((128, 128), F32)],
        moved=5 << 20,
    )(rows, words, meta, quarter)
    recv = lax.all_to_all(sent.reshape(128, CH, 128), BOTH, 0, 0, tiled=True).reshape(128 * CH, 128)

    fresh = call(
        sums_body, jax.ShapeDtypeStruct((32, 8, 128), F32), [pltpu.VMEM((256, 256), F32)], flops=1 << 33, moved=3 << 20
    )(recv)
    owned = lax.all_to_all(
        jnp.broadcast_to(fresh[:, None], (32, 4, 8, 128)).reshape(128, 8, 128), BOTH, 0, 0, tiled=True
    )

    old = lax.dynamic_slice(codebook, (0, 6 * me), (256, 6)).T.reshape(6, 4, 64).transpose(1, 0, 2)
    old = jnp.pad(jnp.concatenate([old, old], 2), ((0, 0), (0, 2), (0, 0)))
    smem = pl.BlockSpec(memory_space=pltpu.SMEM)
    vmem = pl.BlockSpec(memory_space=pltpu.VMEM)
    params = pltpu.CompilerParams(vmem_limit_bytes=VMEM_LIMIT)
    resid, table, shown = pl.pallas_call(
        resid_body,
        in_specs=[smem, vmem, vmem, vmem],
        out_shape=(
            jax.ShapeDtypeStruct((512, 8, 128), F32),
            jax.ShapeDtypeStruct((4, 8, 128), F32),
            jax.ShapeDtypeStruct((2, 8, 128), F32),
        ),
        scratch_shapes=[pltpu.VMEM((256, 256), BF16), pltpu.VMEM((64, 128), F32)],
        compiler_params=params,
        cost_estimate=pl.CostEstimate(flops=1 << 33, bytes_accessed=5 << 20, transcendentals=0),
    )(first, recv, fresh, old)
    books = lax.all_to_all(jnp.broadcast_to(shown.reshape(1, 16, 128), (128, 16, 128)), BOTH, 0, 0, tiled=True)

    errors = pl.pallas_call(
        error_body,
        in_specs=[smem, vmem, vmem, vmem],
        out_shape=jax.ShapeDtypeStruct((128 * 48, 128), F32),
        scratch_shapes=[
            pltpu.VMEM((512, 8, 128), F32),
            pltpu.VMEM((8, 64, 512), F32),
            pltpu.VMEM((64, 128), BF16),
        ],
        compiler_params=params,
        cost_estimate=pl.CostEstimate(flops=1 << 32, bytes_accessed=8 << 20, transcendentals=0),
    )(first, recv, resid, table)
    landed = lax.all_to_all(errors.reshape(128, 48, 128), BOTH, 0, 0, tiled=True).reshape(128 * 48, 128)

    turned = [pltpu.VMEM((768, 128), F32)]
    new_centroids = call(
        lambda *refs: columns_body(1, *refs), jax.ShapeDtypeStruct((128, 768), F32), turned, moved=1 << 20
    )(owned.reshape(1024, 128))
    new_codebook = call(
        lambda *refs: columns_body(2, *refs), jax.ShapeDtypeStruct((256, 768), F32), turned, moved=2 << 20
    )(books.reshape(2048, 128))
    moved_error = call(
        place_body, jax.ShapeDtypeStruct((128, 8, 768), BF16), [pltpu.VMEM((6, 1024, 128), F32)], moved=5 << 20
    )(landed)
    return (new_centroids, moved_error, new_codebook)


def solution(mesh):
    in_specs = (
        P(BOTH, None, None),
        P(BOTH),
        P(BOTH, None),
        P(BOTH, None),
        P(BOTH, None, None),
        P("shard", None),
        P(),
    )
    out_specs = (P("shard", None), P(BOTH, None, None), P())
    return jax.shard_map(local, mesh=mesh, in_specs=in_specs, out_specs=out_specs, check_vma=False)
```

```python
import jax
import jax.numpy as jnp
from jax import lax
from jax.experimental import pallas as pl
from jax.experimental.pallas import tpu as pltpu
from jax.sharding import PartitionSpec as P

PRIOR = 8.0
BOTH = ("shard", "grp")
F32 = jnp.float32
BF16 = jnp.bfloat16

CH = 40
FIRST = (0, 0, 1, 2)
SECOND = (0, 1, 2, 2)


def call(body, out, scratch, mib, scalar=False, operands=1, flops=0, moved=0):
    vmem = pl.BlockSpec(memory_space=pltpu.VMEM)
    return pl.pallas_call(
        body,
        in_specs=([pl.BlockSpec(memory_space=pltpu.SMEM)] if scalar else []) + [vmem] * operands,
        out_shape=out,
        scratch_shapes=list(scratch),
        compiler_params=pltpu.CompilerParams(vmem_limit_bytes=mib << 20),
        cost_estimate=pl.CostEstimate(flops=flops, bytes_accessed=moved, transcendentals=0),
    )


def nt(a, b):
    return lax.dot_general(a, b, (((1,), (1,)), ((), ())), preferred_element_type=F32)


def nn(a, b):
    return lax.dot_general(a, b, (((1,), (0,)), ((), ())), preferred_element_type=F32)


def lanes(shape):
    return lax.broadcasted_iota(jnp.int32, shape, len(shape) - 1)


def subs(shape):
    return lax.broadcasted_iota(jnp.int32, shape, len(shape) - 2)


def split(x):
    hi = x.astype(BF16).astype(F32)
    return hi, x - hi


def send_body(place, corpus, codes, meta, cent, out, turned, words, rows_s, codes_s, rows_c):
    codes_s[:, 0:96] = codes[...].astype(F32)
    for w in range(6):
        rows_c[w] = corpus[:, w * 128 : (w + 1) * 128]
    for p in range(4):
        for w in range(6):
            for h in range(2):
                rows_s[h * 64 : (h + 1) * 64, :] = rows_c[w, pl.ds(2 * p + h, 64, stride=8), :]
            turned[w * 128 : (w + 1) * 128, :] = rows_s[...].T
        for c in range(6):
            out[pl.ds(p * 8 + c, 128, stride=CH), :] = turned[pl.ds(c, 128, stride=6), :]
        for h in range(2):
            rows_s[h * 64 : (h + 1) * 64, :] = codes_s[pl.ds(2 * p + h, 64, stride=8), :]
        words[...] = rows_s[...].T
        for j in range(4):
            for k, pick in ((6, FIRST[j]), (7, SECOND[j])):
                out[pl.ds(j * CH + p * 8 + k, 32, stride=4 * CH), :] = words[pl.ds(pick, 32, stride=3), :]
    for k in range(5):
        out[pl.ds(32 + k, 128, stride=CH), :] = jnp.broadcast_to(meta[k : k + 1, :], (128, 128))
    start = pl.multiple_of(place[1] * 32, 32)
    for w in range(6):
        rows_s[0:32, :] = cent[pl.ds(start, 32), w * 128 : (w + 1) * 128]
        rows_s[32:128, :] = jnp.zeros((96, 128), F32)
        turned[w * 128 : (w + 1) * 128, :] = rows_s[...].T
    parts = [turned[pl.ds(c, 128, stride=6), :] for c in range(6)]
    for k, cols in ((5, (0, 1, 2, 3)), (6, (4, 5))):
        row = parts[cols[0]]
        for i, c in enumerate(cols[1:], 1):
            row = row + pltpu.roll(parts[c], 32 * i, 1)
        out[pl.ds(32 + k, 128, stride=CH), :] = row
    out[pl.ds(39, 128, stride=CH), :] = jnp.zeros((128, 128), F32)


def row_info(tile):
    lane = lanes((8, 128))
    counts = tile[4:5, :]
    counts = jnp.where(lane[0:1] < 64, pltpu.roll(counts, 64, 1), counts)
    place = 2 * subs((8, 128)) + (lane >= 64).astype(jnp.int32)
    used = place < counts.astype(jnp.int32)
    return tile.astype(jnp.int32), used


GRP_SRC = 32
RES_SRC = 16
LOOK_SRC = 8


def sums_body(recv, out, acc):
    acc[...] = jnp.zeros((256, 256), F32)
    sub8 = subs((8, 128))
    digits = subs((256, 128)).astype(F32).astype(BF16)

    def step(i, carry):
        left, right = [], []
        for k in range(GRP_SRC):
            base = pl.multiple_of((i * GRP_SRC + k) * CH, 8)
            label, used = row_info(recv[pl.ds(base + 32, 8), :])
            low = jnp.where(used, label & 255, -1).astype(F32).astype(BF16)
            high = (label >> 8).astype(F32).astype(BF16)
            for p in range(4):
                x = recv[pl.ds(base + 8 * p, 8), :]
                hi, lo = split(x)
                hi = jnp.where(sub8 < 6, hi, jnp.where(sub8 == 6, 1.0, 0.0))
                lo = jnp.where(sub8 < 6, lo, 0.0)
                xb = jnp.concatenate([hi, lo], 0).astype(BF16)
                sel = jnp.broadcast_to(high[p : p + 1, :], (16, 128))
                left.append(
                    jnp.concatenate([jnp.where(sel == jnp.asarray(v, BF16), xb, jnp.zeros_like(xb)) for v in range(16)], 0)
                )
                right.append(jnp.where(digits == jnp.broadcast_to(low[p : p + 1, :], (256, 128)),
                                       jnp.ones((256, 128), BF16), jnp.zeros((256, 128), BF16)))
        acc[...] += nt(jnp.concatenate(left, 1), jnp.concatenate(right, 1))
        return carry

    lax.fori_loop(0, 128 // GRP_SRC, step, 0)

    lane = lanes((8, 128))

    def finish(s, carry):
        sel = s // 2
        old = jnp.zeros((8, 128), F32)
        for g in range(4):
            tile = recv[pl.ds(pl.multiple_of((s * 4 + g) * CH + 32, 8), 8), :]
            both = jnp.where(sub8 < 4, jnp.broadcast_to(tile[5:6, :], (8, 128)), jnp.broadcast_to(tile[6:7, :], (8, 128)))
            moved = jnp.zeros((8, 128), F32)
            for c in range(4):
                moved = jnp.where((sub8 & 3) == c, pltpu.roll(both, (32 * (g - c)) % 128, 1), moved)
            old = jnp.where((lane >> 5) == g, moved, old)
        old = jnp.where(sub8 < 6, old, 0.0)
        rows = acc[pl.ds(pl.multiple_of(sel * 16, 16), 16), :]
        rows = jnp.where((s & 1) == 0, rows[:, :128], rows[:, 128:])
        total = rows[0:8] + rows[8:16]
        count = jnp.broadcast_to(total[6:7, :], (8, 128))
        fresh = (total + PRIOR * old) / (count + PRIOR)
        out[s] = jnp.where(sub8 < 6, fresh, 0.0)
        return carry

    lax.fori_loop(0, 32, finish, 0)


def code_digits(x, first, second_cols, used):
    a = jnp.broadcast_to(x[6:7, :], (8, 128))
    b = jnp.broadcast_to(x[7:8, :], (8, 128))
    return a, b


def resid_body(place, recv, fresh, book, resid, table, share, left, acc):
    first = place[0]
    sub8 = subs((8, 128))
    lane = lanes((8, 128))
    digits = subs((256, 128)).astype(F32).astype(BF16)
    digit64 = subs((64, 128)).astype(F32).astype(BF16)
    for sel in range(16):
        for h in range(2):
            hi, lo = split(fresh[2 * sel + h])
            left[sel * 16 : (sel + 1) * 16, h * 128 : (h + 1) * 128] = jnp.concatenate([hi, lo], 0).astype(BF16)
    acc[...] = jnp.zeros((64, 128), F32)
    one, zero = jnp.ones((), BF16), jnp.zeros((), BF16)
    is_first = (sub8 < first) | (sub8 == 6)

    def step(i, carry):
        lhs, rhs = [], []
        for k in range(RES_SRC):
            src = i * RES_SRC + k
            base = pl.multiple_of(src * CH, 8)
            label, used = row_info(recv[pl.ds(base + 32, 8), :])
            low = (label & 255).astype(F32).astype(BF16)
            high = label >> 8
            hot = [jnp.where(digits == jnp.broadcast_to(low[p : p + 1, :], (256, 128)),
                             jnp.ones((256, 128), BF16), jnp.zeros((256, 128), BF16)) for p in range(4)]
            got = nn(left[...], jnp.concatenate(hot, 1))
            for p in range(4):
                x = recv[pl.ds(base + 8 * p, 8), :]
                sel = jnp.broadcast_to(high[p : p + 1, :], (8, 128))
                ghi = jnp.zeros((8, 128), F32)
                glo = jnp.zeros((8, 128), F32)
                for v in range(16):
                    hit = sel == v
                    ghi = jnp.where(hit, got[v * 16 : v * 16 + 8, p * 128 : (p + 1) * 128], ghi)
                    glo = jnp.where(hit, got[v * 16 + 8 : v * 16 + 16, p * 128 : (p + 1) * 128], glo)
                r = x - (ghi + glo)
                resid[src * 4 + p] = r
                a = jnp.broadcast_to(x[6:7, :], (8, 128))
                b = jnp.broadcast_to(x[7:8, :], (8, 128))
                code = jnp.where(is_first, a, b).astype(jnp.int32)
                use = used[p : p + 1, :]
                pick = jnp.where(jnp.broadcast_to(use, (8, 128)), code >> 6, -1).astype(F32)
                pick = jnp.concatenate([pick, pick], 0).astype(BF16)
                hi, lo = split(r)
                hi = jnp.where(sub8 < 6, hi, 1.0)
                lo = jnp.where(sub8 < 6, lo, 0.0)
                rb = jnp.concatenate([hi, lo], 0).astype(BF16)
                lhs.append(jnp.concatenate([jnp.where(pick == jnp.asarray(v, BF16), rb, jnp.zeros_like(rb)) for v in range(4)], 0))
                da = (x[6:7, :].astype(jnp.int32) & 63).astype(F32).astype(BF16)
                db = (x[7:8, :].astype(jnp.int32) & 63).astype(F32).astype(BF16)
                rhs.append(jnp.concatenate(
                    [jnp.where(digit64 == jnp.broadcast_to(d, (64, 128)), jnp.ones((64, 128), BF16), jnp.zeros((64, 128), BF16))
                     for d in (da, db)], 0))
        acc[...] += nt(jnp.concatenate(lhs, 1), jnp.concatenate(rhs, 1))
        return carry

    lax.fori_loop(0, 128 // RES_SRC, step, 0)

    valid = ((sub8 < first) == (lane < 64)) & (sub8 < 6)
    made = []
    for sel in range(4):
        total = acc[sel * 16 : sel * 16 + 8, :] + acc[sel * 16 + 8 : sel * 16 + 16, :]
        count = jnp.where(lane < 64, jnp.broadcast_to(total[6:7, :], (8, 128)), jnp.broadcast_to(total[7:8, :], (8, 128)))
        new = (total + PRIOR * book[sel]) / (count + PRIOR)
        new = jnp.where(valid, new, 0.0)
        table[sel] = new
        made.append(new + pltpu.roll(new, 64, 1))
    shown = [jnp.where(lane < 64, made[0], made[1]), jnp.where(lane < 64, made[2], made[3])]

    def spread(s, carry):
        for g in range(4):
            share[s * 4 + g, 0:8, :] = fresh[s]
            share[s * 4 + g, 8:16, :] = shown[0]
            share[s * 4 + g, 16:24, :] = shown[1]
        return carry

    lax.fori_loop(0, 32, spread, 0)


def error_body(place, recv, resid, table, out, left, spread, mixed):
    first = place[0]
    sub8 = subs((8, 128))
    lane = lanes((8, 128))
    digit64 = subs((64, 128)).astype(F32).astype(BF16)
    is_first = sub8 < first
    for sel in range(4):
        hi, lo = split(table[sel])
        left[sel * 16 : (sel + 1) * 16, :] = jnp.concatenate([hi, lo], 0).astype(BF16)
    spread[...] = jnp.zeros(spread.shape, BF16)

    def look(i, carry):
        hot, useds = [], []
        for k in range(8):
            src = i * 8 + k
            base = pl.multiple_of(src * CH, 8)
            unused, used = row_info(recv[pl.ds(base + 32, 8), :])
            useds.append(used)
            for p in range(4):
                r = resid[src * 4 + p]
                da = (r[6:7, :].astype(jnp.int32) & 63).astype(F32).astype(BF16)
                db = (r[7:8, :].astype(jnp.int32) & 63).astype(F32).astype(BF16)
                hot.append(jnp.concatenate(
                    [jnp.where(digit64 == jnp.broadcast_to(d, (64, 128)), jnp.ones((64, 128), BF16), jnp.zeros((64, 128), BF16))
                     for d in (da, db)], 0))
        got = nn(left[...], jnp.concatenate(hot, 1))
        errs = []
        for k in range(8):
            src = i * 8 + k
            for p in range(4):
                q = (k * 4 + p) * 128
                r = resid[src * 4 + p]
                a = jnp.broadcast_to(r[6:7, :], (8, 128))
                b = jnp.broadcast_to(r[7:8, :], (8, 128))
                pick = jnp.where(is_first, a, b).astype(jnp.int32) >> 6
                whi = jnp.zeros((8, 128), F32)
                wlo = jnp.zeros((8, 128), F32)
                for v in range(4):
                    hit = pick == v
                    whi = jnp.where(hit, got[v * 16 : v * 16 + 8, q : q + 128], whi)
                    wlo = jnp.where(hit, got[v * 16 + 8 : v * 16 + 16, q : q + 128], wlo)
                errs.append(jnp.where(jnp.broadcast_to(useds[k][p : p + 1, :], (8, 128)) & (sub8 < 6), r - (whi + wlo), 0.0))
        for g in range(4):
            rows = []
            for p in range(4):
                e0, e1 = errs[g * 4 + p], errs[(g + 4) * 4 + p]
                rows.append(jnp.where(lane < 64, e0, pltpu.roll(e1, 64, 1)))
                rows.append(jnp.where(lane < 64, pltpu.roll(e0, 64, 1), e1))
            spread[i, g * 64 : (g + 1) * 64, g * 128 : (g + 1) * 128] = jnp.concatenate(rows, 0).astype(BF16)
        return carry

    lax.fori_loop(0, 16, look, 0)

    spots = subs((256, 128)).astype(F32).astype(BF16)
    spot_lane = lanes((1, 128))

    def mix(sh, carry):
        total = jnp.zeros((512, 256), F32)
        hots, errs = [], []
        for pair in range(2):
            cols = []
            for g in range(4):
                aims = []
                for q in range(2):
                    src = sh * 16 + (2 * pair + q) * 4 + g
                    row = recv[pl.ds(src * CH + 36, 1), :].astype(jnp.int32)
                    aims.append((row >> 2) * 16 + (row & 3) + (2 * pair + q) * 4)
                aim = jnp.where(spot_lane < 64, aims[0], pltpu.roll(aims[1], 64, 1))
                halves = []
                for h in range(2):
                    at = jnp.broadcast_to((aim - 256 * h).astype(F32).astype(BF16), (256, 128))
                    halves.append(jnp.where(spots == at, jnp.ones((256, 128), BF16), jnp.zeros((256, 128), BF16)))
                cols.append(jnp.concatenate(halves, 0))
            hots.append(jnp.concatenate(cols, 1))
            errs.append(spread[sh * 2 + pair])
        got = nt(jnp.concatenate(hots, 1), jnp.concatenate(errs, 1))
        mixed[:, pl.ds(sh * 16, 16), :] = got.reshape(32, 16, 256)
        return carry

    lax.fori_loop(0, 8, mix, 0)

    def finish(t, carry):
        for h in range(2):
            tile = mixed[t, :, h * 128 : (h + 1) * 128].T
            for g2 in range(2):
                for r in range(8):
                    out[pl.ds((t * 4 + 2 * h + g2) * 48 + r, 6, stride=8), :] = tile[g2 * 64 + r * 8 : g2 * 64 + r * 8 + 6, :]
        return carry

    lax.fori_loop(0, 32, finish, 0)


def place_body(recv, out, turned):
    for r in range(8):
        for w in range(6):
            turned[w, pl.ds(r, 128, stride=8), :] = recv[pl.ds(w * 1024 + r, 128, stride=8), :].T
    for w in range(6):
        out[:, :, w * 128 : (w + 1) * 128] = turned[w].reshape(128, 8, 128).astype(BF16)


def columns_body(recv, centroids, book, turned):
    for h in range(3):
        for c in range(6):
            turned[pl.ds(c, 128, stride=6), :] = recv[pl.ds(h * 8 + c, 128, stride=24), :]
        for w in range(6):
            tile = turned[w * 128 : (w + 1) * 128, :].T
            if h == 0:
                centroids[:, w * 128 : (w + 1) * 128] = tile
            else:
                book[(h - 1) * 128 : h * 128, w * 128 : (w + 1) * 128] = tile


def slot_ranks(dest):
    count = dest.shape[0]
    order = jnp.arange(count, dtype=jnp.int32)
    same = (dest[:, None] == dest[None, :]) & (order[None, :] < order[:, None])
    return jnp.sum(same.astype(jnp.int32), axis=1)


def local(corpus, block_rows, targets, assign, codes, centroids, codebook):
    grp = lax.axis_index("grp")
    me = lax.axis_index("shard") * 4 + grp
    first = jnp.where(grp == 1, 2, jnp.where(grp == 2, 4, 6)).astype(jnp.int32)
    dest = targets[:, 0]
    slot = dest * 4 + slot_ranks(dest)
    meta = jnp.concatenate(
        [assign.T.reshape(4, 128), jnp.concatenate([slot, block_rows]).reshape(1, 128), jnp.zeros((3, 128), jnp.int32)], 0
    ).astype(F32)
    place = jnp.stack([first, grp])

    sent = call(
        send_body,
        jax.ShapeDtypeStruct((128 * CH, 128), F32),
        [pltpu.VMEM((768, 128), F32), pltpu.VMEM((128, 128), F32), pltpu.VMEM((128, 128), F32), pltpu.VMEM((512, 128), F32),
         pltpu.VMEM((6, 512, 128), F32)],
        16,
        scalar=True,
        operands=4,
        moved=5 << 20,
    )(place, corpus.reshape(512, 768), codes.reshape(512, 96), meta, centroids)
    recv = lax.all_to_all(sent.reshape(128, CH, 128), BOTH, 0, 0, tiled=True).reshape(128 * CH, 128)

    fresh = call(
        sums_body,
        jax.ShapeDtypeStruct((32, 8, 128), F32),
        [pltpu.VMEM((256, 256), F32)],
        12,
        flops=1 << 33,
        moved=3 << 20,
    )(recv)

    old = lax.dynamic_slice(codebook, (0, 6 * me), (256, 6)).T.reshape(6, 4, 64).transpose(1, 0, 2)
    old = jnp.pad(jnp.concatenate([old, old], 2), ((0, 0), (0, 2), (0, 0)))
    resid, table, share = call(
        resid_body,
        (
            jax.ShapeDtypeStruct((512, 8, 128), F32),
            jax.ShapeDtypeStruct((4, 8, 128), F32),
            jax.ShapeDtypeStruct((128, 24, 128), F32),
        ),
        [pltpu.VMEM((256, 256), BF16), pltpu.VMEM((64, 128), F32)],
        16,
        scalar=True,
        operands=3,
        flops=1 << 33,
        moved=6 << 20,
    )(place, recv, fresh, old)
    shared = lax.all_to_all(share, BOTH, 0, 0, tiled=True).reshape(128 * 24, 128)

    errors = call(
        error_body,
        jax.ShapeDtypeStruct((128 * 48, 128), F32),
        [pltpu.VMEM((64, 128), BF16), pltpu.VMEM((16, 256, 512), BF16), pltpu.VMEM((32, 128, 256), F32)],
        24,
        scalar=True,
        operands=3,
        flops=1 << 33,
        moved=8 << 20,
    )(place, recv, resid, table)
    landed = lax.all_to_all(errors.reshape(128, 48, 128), BOTH, 0, 0, tiled=True).reshape(128 * 48, 128)

    new_centroids, new_codebook = call(
        columns_body,
        (jax.ShapeDtypeStruct((128, 768), F32), jax.ShapeDtypeStruct((256, 768), F32)),
        [pltpu.VMEM((768, 128), F32)],
        12,
        moved=3 << 20,
    )(shared)
    moved_error = call(
        place_body, jax.ShapeDtypeStruct((128, 8, 768), BF16), [pltpu.VMEM((6, 1024, 128), F32)], 16, moved=5 << 20
    )(landed)
    return (new_centroids, moved_error, new_codebook)


def solution(mesh):
    in_specs = (
        P(BOTH, None, None),
        P(BOTH),
        P(BOTH, None),
        P(BOTH, None),
        P(BOTH, None, None),
        P("shard", None),
        P(),
    )
    out_specs = (P("shard", None), P(BOTH, None, None), P())
    return jax.shard_map(local, mesh=mesh, in_specs=in_specs, out_specs=out_specs, check_vma=False)
```

```python
import jax
import jax.numpy as jnp
from jax import lax
from jax.experimental import pallas as pl
from jax.experimental.pallas import tpu as pltpu
from jax.sharding import PartitionSpec as P

PRIOR = 8.0
BOTH = ("shard", "grp")
F32 = jnp.float32
BF16 = jnp.bfloat16

CH = 40
EC = 72
FIRST = (0, 0, 1, 2)
SECOND = (0, 1, 2, 2)


def call(body, ins, outs, out, scratch, mib, flops=0, moved=0):
    return pl.pallas_call(
        body,
        in_specs=ins,
        out_specs=outs,
        out_shape=out,
        scratch_shapes=list(scratch),
        compiler_params=pltpu.CompilerParams(vmem_limit_bytes=mib << 20),
        cost_estimate=pl.CostEstimate(flops=flops, bytes_accessed=moved, transcendentals=0),
    )


def nt(a, b):
    return lax.dot_general(a, b, (((1,), (1,)), ((), ())), preferred_element_type=F32)


def nn(a, b):
    return lax.dot_general(a, b, (((1,), (0,)), ((), ())), preferred_element_type=F32)


def lanes(shape):
    return lax.broadcasted_iota(jnp.int32, shape, len(shape) - 1)


def subs(shape):
    return lax.broadcasted_iota(jnp.int32, shape, len(shape) - 2)


def split(x):
    hi = x.astype(BF16).astype(F32)
    return hi, x - hi


def send_body(place, corpus, codes, cent, dest, counts, assign, out, turned, words, rows_s, codes_s, rows_c, codes_i, cent_s, sems):
    moves = [pltpu.make_async_copy(corpus.at[:, pl.ds(w * 128, 128)], rows_c.at[w], sems.at[w]) for w in range(6)]
    moves.append(pltpu.make_async_copy(codes, codes_i, sems.at[6]))
    moves.append(pltpu.make_async_copy(cent, cent_s, sems.at[7]))
    for move in moves:
        move.start()
    lane = lanes((1, 128))
    here = dest[...].astype(F32)
    here = jnp.broadcast_to(jnp.concatenate([here, here], 1), (128, 128))
    there = here.T
    before = (there == here) & (subs((128, 128)) < lanes((128, 128)))
    rank = jnp.sum(jnp.where(before, 1.0, 0.0), axis=0, keepdims=True)
    slot = here[0:1, :] * 4.0 + rank
    used = counts[...].astype(F32)
    used = jnp.concatenate([used, used], 1)
    labels = assign[...].astype(F32)
    labels = jnp.concatenate([labels, labels], 1)
    infos = [jnp.where(lane < 64, labels[2 * p : 2 * p + 1, :], labels[2 * p + 1 : 2 * p + 2, :]) for p in range(4)]
    infos.append(jnp.where(lane < 64, slot, used))
    for k in range(5):
        out[pl.ds(32 + k, 128, stride=CH), :] = jnp.broadcast_to(infos[k], (128, 128))
    out[pl.ds(39, 128, stride=CH), :] = jnp.zeros((128, 128), F32)
    moves[6].wait()
    codes_s[:, 0:96] = codes_i[...].astype(F32)
    codes_s[:, 96:128] = jnp.zeros((512, 32), F32)
    moves[7].wait()
    start = pl.multiple_of(place[1] * 32, 32)
    for w in range(6):
        rows_s[0:32, :] = cent_s[pl.ds(start, 32), w * 128 : (w + 1) * 128]
        rows_s[32:128, :] = jnp.zeros((96, 128), F32)
        turned[w * 128 : (w + 1) * 128, :] = rows_s[...].T
    parts = [turned[pl.ds(c, 128, stride=6), :] for c in range(6)]
    for k, cols in ((5, (0, 1, 2, 3)), (6, (4, 5))):
        row = parts[cols[0]]
        for i, c in enumerate(cols[1:], 1):
            row = row + pltpu.roll(parts[c], 32 * i, 1)
        out[pl.ds(32 + k, 128, stride=CH), :] = row
    for p in range(4):
        for h in range(2):
            rows_s[h * 64 : (h + 1) * 64, :] = codes_s[pl.ds(2 * p + h, 64, stride=8), :]
        words[...] = rows_s[...].T
        for j in range(4):
            for k, pick in ((6, FIRST[j]), (7, SECOND[j])):
                out[pl.ds(j * CH + p * 8 + k, 32, stride=4 * CH), :] = words[pl.ds(pick, 32, stride=3), :]
        for w in range(6):
            if p == 0:
                moves[w].wait()
            for h in range(2):
                rows_s[h * 64 : (h + 1) * 64, :] = rows_c[w, pl.ds(2 * p + h, 64, stride=8), :]
            turned[w * 128 : (w + 1) * 128, :] = rows_s[...].T
        for c in range(6):
            out[pl.ds(p * 8 + c, 128, stride=CH), :] = turned[pl.ds(c, 128, stride=6), :]


def row_info(tile):
    lane = lanes((8, 128))
    counts = tile[4:5, :]
    counts = jnp.where(lane[0:1] < 64, pltpu.roll(counts, 64, 1), counts)
    place = 2 * subs((8, 128)) + (lane >= 64).astype(jnp.int32)
    used = place < counts.astype(jnp.int32)
    return tile.astype(jnp.int32), used


GRP_SRC = 32
RES_SRC = 16
LOOK_SRC = 8


def sums_part(recv, out, acc):
    acc[...] = jnp.zeros((256, 256), F32)
    sub8 = subs((8, 128))
    digits = subs((256, 128)).astype(F32).astype(BF16)

    def step(i, carry):
        left, right = [], []
        for k in range(GRP_SRC):
            base = pl.multiple_of((i * GRP_SRC + k) * CH, 8)
            label, used = row_info(recv[pl.ds(base + 32, 8), :])
            low = jnp.where(used, label & 255, -1).astype(F32).astype(BF16)
            high = (label >> 8).astype(F32).astype(BF16)
            for p in range(4):
                x = recv[pl.ds(base + 8 * p, 8), :]
                hi, lo = split(x)
                hi = jnp.where(sub8 < 6, hi, jnp.where(sub8 == 6, 1.0, 0.0))
                lo = jnp.where(sub8 < 6, lo, 0.0)
                xb = jnp.concatenate([hi, lo], 0).astype(BF16)
                sel = jnp.broadcast_to(high[p : p + 1, :], (16, 128))
                left.append(
                    jnp.concatenate([jnp.where(sel == jnp.asarray(v, BF16), xb, jnp.zeros_like(xb)) for v in range(16)], 0)
                )
                right.append(jnp.where(digits == jnp.broadcast_to(low[p : p + 1, :], (256, 128)),
                                       jnp.ones((256, 128), BF16), jnp.zeros((256, 128), BF16)))
        acc[...] += nt(jnp.concatenate(left, 1), jnp.concatenate(right, 1))
        return carry

    lax.fori_loop(0, 128 // GRP_SRC, step, 0)

    lane = lanes((8, 128))

    def finish(s, carry):
        sel = s // 2
        old = jnp.zeros((8, 128), F32)
        for g in range(4):
            tile = recv[pl.ds(pl.multiple_of((s * 4 + g) * CH + 32, 8), 8), :]
            both = jnp.where(sub8 < 4, jnp.broadcast_to(tile[5:6, :], (8, 128)), jnp.broadcast_to(tile[6:7, :], (8, 128)))
            moved = jnp.zeros((8, 128), F32)
            for c in range(4):
                moved = jnp.where((sub8 & 3) == c, pltpu.roll(both, (32 * (g - c)) % 128, 1), moved)
            old = jnp.where((lane >> 5) == g, moved, old)
        old = jnp.where(sub8 < 6, old, 0.0)
        rows = acc[pl.ds(pl.multiple_of(sel * 16, 16), 16), :]
        rows = jnp.where((s & 1) == 0, rows[:, :128], rows[:, 128:])
        total = rows[0:8] + rows[8:16]
        count = jnp.broadcast_to(total[6:7, :], (8, 128))
        fresh = (total + PRIOR * old) / (count + PRIOR)
        out[s] = jnp.where(sub8 < 6, fresh, 0.0)
        return carry

    lax.fori_loop(0, 32, finish, 0)


def code_digits(x, first, second_cols, used):
    a = jnp.broadcast_to(x[6:7, :], (8, 128))
    b = jnp.broadcast_to(x[7:8, :], (8, 128))
    return a, b


def resid_part(place, recv, fresh, book, resid, table, left, acc):
    first = place[0]
    sub8 = subs((8, 128))
    lane = lanes((8, 128))
    digits = subs((256, 128)).astype(F32).astype(BF16)
    digit64 = subs((64, 128)).astype(F32).astype(BF16)
    for sel in range(16):
        for h in range(2):
            hi, lo = split(fresh[2 * sel + h])
            left[sel * 16 : (sel + 1) * 16, h * 128 : (h + 1) * 128] = jnp.concatenate([hi, lo], 0).astype(BF16)
    acc[...] = jnp.zeros((64, 128), F32)
    one, zero = jnp.ones((), BF16), jnp.zeros((), BF16)
    is_first = (sub8 < first) | (sub8 == 6)

    def step(i, carry):
        lhs, rhs = [], []
        for k in range(RES_SRC):
            src = i * RES_SRC + k
            base = pl.multiple_of(src * CH, 8)
            label, used = row_info(recv[pl.ds(base + 32, 8), :])
            low = (label & 255).astype(F32).astype(BF16)
            high = label >> 8
            hot = [jnp.where(digits == jnp.broadcast_to(low[p : p + 1, :], (256, 128)),
                             jnp.ones((256, 128), BF16), jnp.zeros((256, 128), BF16)) for p in range(4)]
            got = nn(left[...], jnp.concatenate(hot, 1))
            for p in range(4):
                x = recv[pl.ds(base + 8 * p, 8), :]
                sel = jnp.broadcast_to(high[p : p + 1, :], (8, 128))
                ghi = jnp.zeros((8, 128), F32)
                glo = jnp.zeros((8, 128), F32)
                for v in range(16):
                    hit = sel == v
                    ghi = jnp.where(hit, got[v * 16 : v * 16 + 8, p * 128 : (p + 1) * 128], ghi)
                    glo = jnp.where(hit, got[v * 16 + 8 : v * 16 + 16, p * 128 : (p + 1) * 128], glo)
                r = x - (ghi + glo)
                resid[src * 4 + p] = r
                a = jnp.broadcast_to(x[6:7, :], (8, 128))
                b = jnp.broadcast_to(x[7:8, :], (8, 128))
                code = jnp.where(is_first, a, b).astype(jnp.int32)
                use = used[p : p + 1, :]
                pick = jnp.where(jnp.broadcast_to(use, (8, 128)), code >> 6, -1).astype(F32)
                pick = jnp.concatenate([pick, pick], 0).astype(BF16)
                hi, lo = split(r)
                hi = jnp.where(sub8 < 6, hi, 1.0)
                lo = jnp.where(sub8 < 6, lo, 0.0)
                rb = jnp.concatenate([hi, lo], 0).astype(BF16)
                lhs.append(jnp.concatenate([jnp.where(pick == jnp.asarray(v, BF16), rb, jnp.zeros_like(rb)) for v in range(4)], 0))
                da = (x[6:7, :].astype(jnp.int32) & 63).astype(F32).astype(BF16)
                db = (x[7:8, :].astype(jnp.int32) & 63).astype(F32).astype(BF16)
                rhs.append(jnp.concatenate(
                    [jnp.where(digit64 == jnp.broadcast_to(d, (64, 128)), jnp.ones((64, 128), BF16), jnp.zeros((64, 128), BF16))
                     for d in (da, db)], 0))
        acc[...] += nt(jnp.concatenate(lhs, 1), jnp.concatenate(rhs, 1))
        return carry

    lax.fori_loop(0, 128 // RES_SRC, step, 0)

    valid = ((sub8 < first) == (lane < 64)) & (sub8 < 6)
    made = []
    for sel in range(4):
        total = acc[sel * 16 : sel * 16 + 8, :] + acc[sel * 16 + 8 : sel * 16 + 16, :]
        count = jnp.where(lane < 64, jnp.broadcast_to(total[6:7, :], (8, 128)), jnp.broadcast_to(total[7:8, :], (8, 128)))
        new = (total + PRIOR * book[sel]) / (count + PRIOR)
        new = jnp.where(valid, new, 0.0)
        table[sel] = new
        made.append(new + pltpu.roll(new, 64, 1))
    shown = [jnp.where(lane < 64, made[0], made[1]), jnp.where(lane < 64, made[2], made[3])]

    return shown


def error_part(place, recv, fresh, shown, resid, table, out, left, spread, mixed, stage, sems):
    first = place[0]
    sub8 = subs((8, 128))
    lane = lanes((8, 128))
    digit64 = subs((64, 128)).astype(F32).astype(BF16)
    is_first = sub8 < first
    for sel in range(4):
        hi, lo = split(table[sel])
        left[sel * 16 : (sel + 1) * 16, :] = jnp.concatenate([hi, lo], 0).astype(BF16)
    spread[...] = jnp.zeros(spread.shape, BF16)

    def look(i, carry):
        hot, useds = [], []
        for k in range(8):
            src = i * 8 + k
            base = pl.multiple_of(src * CH, 8)
            unused, used = row_info(recv[pl.ds(base + 32, 8), :])
            useds.append(used)
            for p in range(4):
                r = resid[src * 4 + p]
                da = (r[6:7, :].astype(jnp.int32) & 63).astype(F32).astype(BF16)
                db = (r[7:8, :].astype(jnp.int32) & 63).astype(F32).astype(BF16)
                hot.append(jnp.concatenate(
                    [jnp.where(digit64 == jnp.broadcast_to(d, (64, 128)), jnp.ones((64, 128), BF16), jnp.zeros((64, 128), BF16))
                     for d in (da, db)], 0))
        got = nn(left[...], jnp.concatenate(hot, 1))
        errs = []
        for k in range(8):
            src = i * 8 + k
            for p in range(4):
                q = (k * 4 + p) * 128
                r = resid[src * 4 + p]
                a = jnp.broadcast_to(r[6:7, :], (8, 128))
                b = jnp.broadcast_to(r[7:8, :], (8, 128))
                pick = jnp.where(is_first, a, b).astype(jnp.int32) >> 6
                whi = jnp.zeros((8, 128), F32)
                wlo = jnp.zeros((8, 128), F32)
                for v in range(4):
                    hit = pick == v
                    whi = jnp.where(hit, got[v * 16 : v * 16 + 8, q : q + 128], whi)
                    wlo = jnp.where(hit, got[v * 16 + 8 : v * 16 + 16, q : q + 128], wlo)
                errs.append(jnp.where(jnp.broadcast_to(useds[k][p : p + 1, :], (8, 128)) & (sub8 < 6), r - (whi + wlo), 0.0))
        for g in range(4):
            rows = []
            for p in range(4):
                e0, e1 = errs[g * 4 + p], errs[(g + 4) * 4 + p]
                rows.append(jnp.where(lane < 64, e0, pltpu.roll(e1, 64, 1)))
                rows.append(jnp.where(lane < 64, pltpu.roll(e0, 64, 1), e1))
            spread[i, g * 64 : (g + 1) * 64, g * 128 : (g + 1) * 128] = jnp.concatenate(rows, 0).astype(BF16)
        return carry

    lax.fori_loop(0, 16, look, 0)

    spots = subs((256, 128)).astype(F32).astype(BF16)
    spot_lane = lanes((1, 128))

    def mix(sh, carry):
        total = jnp.zeros((512, 256), F32)
        hots, errs = [], []
        for pair in range(2):
            cols = []
            for g in range(4):
                aims = []
                for q in range(2):
                    src = sh * 16 + (2 * pair + q) * 4 + g
                    row = recv[pl.ds(src * CH + 36, 1), :].astype(jnp.int32)
                    aims.append((row >> 2) * 16 + (row & 3) + (2 * pair + q) * 4)
                aim = jnp.where(spot_lane < 64, aims[0], pltpu.roll(aims[1], 64, 1))
                halves = []
                for h in range(2):
                    at = jnp.broadcast_to((aim - 256 * h).astype(F32).astype(BF16), (256, 128))
                    halves.append(jnp.where(spots == at, jnp.ones((256, 128), BF16), jnp.zeros((256, 128), BF16)))
                cols.append(jnp.concatenate(halves, 0))
            hots.append(jnp.concatenate(cols, 1))
            errs.append(spread[sh * 2 + pair])
        got = nt(jnp.concatenate(hots, 1), jnp.concatenate(errs, 1))
        mixed[:, pl.ds(sh * 16, 16), :] = got.reshape(32, 16, 256)
        return carry

    lax.fori_loop(0, 8, mix, 0)

    def move(t):
        rows = pl.ds(pl.multiple_of(t * 4 * EC, 8), 4 * EC)
        return pltpu.make_async_copy(stage.at[rows], out.at[rows], sems.at[t])

    def finish(t, carry):
        for h in range(2):
            tile = mixed[t, :, h * 128 : (h + 1) * 128].T
            for g2 in range(2):
                base = pl.multiple_of((t * 4 + 2 * h + g2) * EC, 8)
                for r in range(8):
                    stage[pl.ds(base + r, 6, stride=8), :] = tile[g2 * 64 + r * 8 : g2 * 64 + r * 8 + 6, :]
                stage[pl.ds(base + 48, 8), :] = fresh[t]
                stage[pl.ds(base + 56, 8), :] = shown[0]
                stage[pl.ds(base + 64, 8), :] = shown[1]
        move(t).start()
        return carry

    lax.fori_loop(0, 32, finish, 0)

    def settle(t, carry):
        move(t).wait()
        return carry

    lax.fori_loop(0, 32, settle, 0)


def main_body(place, recv, book, out, sums, fresh, left, csum, resid, table, words, spread, mixed, stage, sems):
    sums_part(recv, fresh, sums)
    shown = resid_part(place, recv, fresh, book, resid, table, left, csum)
    error_part(place, recv, fresh, shown, resid, table, out, words, spread, mixed, stage, sems)


def place_body(landed, out, centroids, book, buf, extra, turned, cols, sems):
    moves = [
        pltpu.make_async_copy(landed.at[pl.ds(16 * k, 16), pl.ds(0, 48)], buf.at[pl.ds(16 * k, 16)], sems.at[k])
        for k in range(8)
    ]
    moves.append(pltpu.make_async_copy(landed.at[:, pl.ds(48, 24)], extra, sems.at[8]))
    for move in moves[8:] + moves[:8]:
        move.start()
    moves[8].wait()
    flat = extra.reshape(128 * 24, 128)
    for h in range(3):
        for c in range(6):
            cols[pl.ds(c, 128, stride=6), :] = flat[pl.ds(h * 8 + c, 128, stride=24), :]
        for w in range(6):
            tile = cols[w * 128 : (w + 1) * 128, :].T
            if h == 0:
                centroids[:, w * 128 : (w + 1) * 128] = tile
            else:
                book[(h - 1) * 128 : h * 128, w * 128 : (w + 1) * 128] = tile
    flat = buf.reshape(128 * 48, 128)
    ready = 0
    for w in range(6):
        need = (128 * w + 127) // 6 // 16 + 1
        for k in range(ready, need):
            moves[k].wait()
        ready = need
        for r in range(8):
            turned[w, pl.ds(r, 128, stride=8), :] = flat[pl.ds(w * 1024 + r, 128, stride=8), :].T
        out[:, :, w * 128 : (w + 1) * 128] = turned[w].reshape(128, 8, 128).astype(BF16)


def local(corpus, block_rows, targets, assign, codes, centroids, codebook):
    grp = lax.axis_index("grp")
    me = lax.axis_index("shard") * 4 + grp
    first = jnp.where(grp == 1, 2, jnp.where(grp == 2, 4, 6)).astype(jnp.int32)
    place = jnp.stack([first, grp])
    vmem, hbm, smem = (pl.BlockSpec(memory_space=m) for m in (pltpu.VMEM, pltpu.HBM, pltpu.SMEM))

    sent = call(
        send_body,
        [smem, hbm, hbm, hbm, vmem, vmem, vmem],
        vmem,
        jax.ShapeDtypeStruct((128 * CH, 128), F32),
        [
            pltpu.VMEM((768, 128), F32),
            pltpu.VMEM((128, 128), F32),
            pltpu.VMEM((128, 128), F32),
            pltpu.VMEM((512, 128), F32),
            pltpu.VMEM((6, 512, 128), F32),
            pltpu.VMEM((512, 96), jnp.int32),
            pltpu.VMEM((128, 768), F32),
            pltpu.SemaphoreType.DMA((8,)),
        ],
        16,
        moved=5 << 20,
    )(
        place,
        corpus.reshape(512, 768),
        codes.reshape(512, 96),
        centroids,
        targets.reshape(1, 64),
        block_rows.reshape(1, 64),
        assign.T,
    )
    recv = lax.all_to_all(sent.reshape(128, CH, 128), BOTH, 0, 0, tiled=True).reshape(128 * CH, 128)

    old = lax.dynamic_slice(codebook, (0, 6 * me), (256, 6)).T.reshape(6, 4, 64).transpose(1, 0, 2)
    old = jnp.pad(jnp.concatenate([old, old], 2), ((0, 0), (0, 2), (0, 0)))
    errors = call(
        main_body,
        [smem, vmem, vmem],
        hbm,
        jax.ShapeDtypeStruct((128 * EC, 128), F32),
        [
            pltpu.VMEM((256, 256), F32),
            pltpu.VMEM((32, 8, 128), F32),
            pltpu.VMEM((256, 256), BF16),
            pltpu.VMEM((64, 128), F32),
            pltpu.VMEM((512, 8, 128), F32),
            pltpu.VMEM((4, 8, 128), F32),
            pltpu.VMEM((64, 128), BF16),
            pltpu.VMEM((16, 256, 512), BF16),
            pltpu.VMEM((32, 128, 256), F32),
            pltpu.VMEM((128 * EC, 128), F32),
            pltpu.SemaphoreType.DMA((32,)),
        ],
        32,
        flops=1 << 34,
        moved=8 << 20,
    )(place, recv, old)
    landed = lax.all_to_all(errors.reshape(128, EC, 128), BOTH, 0, 0, tiled=True)

    moved_error, new_centroids, new_codebook = call(
        place_body,
        [hbm],
        (vmem, vmem, vmem),
        (
            jax.ShapeDtypeStruct((128, 8, 768), BF16),
            jax.ShapeDtypeStruct((128, 768), F32),
            jax.ShapeDtypeStruct((256, 768), F32),
        ),
        [
            pltpu.VMEM((128, 48, 128), F32),
            pltpu.VMEM((128, 24, 128), F32),
            pltpu.VMEM((6, 1024, 128), F32),
            pltpu.VMEM((768, 128), F32),
            pltpu.SemaphoreType.DMA((9,)),
        ],
        24,
        moved=7 << 20,
    )(landed)
    return (new_centroids, moved_error, new_codebook)


def solution(mesh):
    in_specs = (
        P(BOTH, None, None),
        P(BOTH),
        P(BOTH, None),
        P(BOTH, None),
        P(BOTH, None, None),
        P("shard", None),
        P(),
    )
    out_specs = (P("shard", None), P(BOTH, None, None), P())
    return jax.shard_map(local, mesh=mesh, in_specs=in_specs, out_specs=out_specs, check_vma=False)
```

```python
import jax
import jax.numpy as jnp
from jax import lax
from jax.experimental import pallas as pl
from jax.experimental.pallas import tpu as pltpu
from jax.sharding import PartitionSpec as P

PRIOR = 8.0
BOTH = ("shard", "grp")
F32 = jnp.float32
BF16 = jnp.bfloat16

CH = 40
EC = 72
FIRST = (0, 0, 1, 2)
SECOND = (0, 1, 2, 2)


def call(body, ins, outs, out, scratch, mib, flops=0, moved=0):
    return pl.pallas_call(
        body,
        in_specs=ins,
        out_specs=outs,
        out_shape=out,
        scratch_shapes=list(scratch),
        compiler_params=pltpu.CompilerParams(vmem_limit_bytes=mib << 20),
        cost_estimate=pl.CostEstimate(flops=flops, bytes_accessed=moved, transcendentals=0),
    )


def nt(a, b):
    return lax.dot_general(a, b, (((1,), (1,)), ((), ())), preferred_element_type=F32)


def nn(a, b):
    return lax.dot_general(a, b, (((1,), (0,)), ((), ())), preferred_element_type=F32)


def lanes(shape):
    return lax.broadcasted_iota(jnp.int32, shape, len(shape) - 1)


def subs(shape):
    return lax.broadcasted_iota(jnp.int32, shape, len(shape) - 2)


def split(x):
    hi = x.astype(BF16).astype(F32)
    return hi, x - hi


def send_body(place, corpus, codes, cent, dest, counts, assign, out, turned, words, rows_s, codes_s, rows_c, codes_i, cent_s, sems):
    moves = [pltpu.make_async_copy(corpus.at[:, pl.ds(w * 128, 128)], rows_c.at[w], sems.at[w]) for w in range(6)]
    moves.append(pltpu.make_async_copy(codes, codes_i, sems.at[6]))
    moves.append(pltpu.make_async_copy(cent, cent_s, sems.at[7]))
    for move in moves:
        move.start()
    lane = lanes((1, 128))
    here = dest[...].astype(F32)
    here = jnp.broadcast_to(jnp.concatenate([here, here], 1), (128, 128))
    there = here.T
    before = (there == here) & (subs((128, 128)) < lanes((128, 128)))
    rank = jnp.sum(jnp.where(before, 1.0, 0.0), axis=0, keepdims=True)
    slot = here[0:1, :] * 4.0 + rank
    used = counts[...].astype(F32)
    used = jnp.concatenate([used, used], 1)
    labels = assign[...].astype(F32)
    labels = jnp.concatenate([labels, labels], 1)
    infos = [jnp.where(lane < 64, labels[2 * p : 2 * p + 1, :], labels[2 * p + 1 : 2 * p + 2, :]) for p in range(4)]
    infos.append(jnp.where(lane < 64, slot, used))
    for k in range(5):
        out[pl.ds(32 + k, 128, stride=CH), :] = jnp.broadcast_to(infos[k], (128, 128))
    out[pl.ds(39, 128, stride=CH), :] = jnp.zeros((128, 128), F32)
    moves[6].wait()
    codes_s[:, 0:96] = codes_i[...].astype(F32)
    codes_s[:, 96:128] = jnp.zeros((512, 32), F32)
    moves[7].wait()
    start = pl.multiple_of(place[1] * 32, 32)
    for w in range(6):
        rows_s[0:32, :] = cent_s[pl.ds(start, 32), w * 128 : (w + 1) * 128]
        rows_s[32:128, :] = jnp.zeros((96, 128), F32)
        turned[w * 128 : (w + 1) * 128, :] = rows_s[...].T
    parts = [turned[pl.ds(c, 128, stride=6), :] for c in range(6)]
    for k, cols in ((5, (0, 1, 2, 3)), (6, (4, 5))):
        row = parts[cols[0]]
        for i, c in enumerate(cols[1:], 1):
            row = row + pltpu.roll(parts[c], 32 * i, 1)
        out[pl.ds(32 + k, 128, stride=CH), :] = row
    for p in range(4):
        for h in range(2):
            rows_s[h * 64 : (h + 1) * 64, :] = codes_s[pl.ds(2 * p + h, 64, stride=8), :]
        words[...] = rows_s[...].T
        for j in range(4):
            for k, pick in ((6, FIRST[j]), (7, SECOND[j])):
                out[pl.ds(j * CH + p * 8 + k, 32, stride=4 * CH), :] = words[pl.ds(pick, 32, stride=3), :]
        for w in range(6):
            if p == 0:
                moves[w].wait()
            for h in range(2):
                rows_s[h * 64 : (h + 1) * 64, :] = rows_c[w, pl.ds(2 * p + h, 64, stride=8), :]
            turned[w * 128 : (w + 1) * 128, :] = rows_s[...].T
        for c in range(6):
            out[pl.ds(p * 8 + c, 128, stride=CH), :] = turned[pl.ds(c, 128, stride=6), :]


def row_info(tile):
    lane = lanes((8, 128))
    counts = tile[4:5, :]
    counts = jnp.where(lane[0:1] < 64, pltpu.roll(counts, 64, 1), counts)
    place = 2 * subs((8, 128)) + (lane >= 64).astype(jnp.int32)
    used = place < counts.astype(jnp.int32)
    return tile.astype(jnp.int32), used


GRP_SRC = 32
RES_SRC = 32
SEND_MIB = 56
LOOK_SRC = 8


def sums_part(recv, out, acc):
    acc[...] = jnp.zeros((256, 256), F32)
    sub8 = subs((8, 128))
    digits = subs((256, 128)).astype(F32).astype(BF16)

    def step(i, carry):
        left, right = [], []
        for k in range(GRP_SRC):
            base = pl.multiple_of((i * GRP_SRC + k) * CH, 8)
            label, used = row_info(recv[pl.ds(base + 32, 8), :])
            low = jnp.where(used, label & 255, -1).astype(F32).astype(BF16)
            high = (label >> 8).astype(F32).astype(BF16)
            for p in range(4):
                x = recv[pl.ds(base + 8 * p, 8), :]
                hi, lo = split(x)
                hi = jnp.where(sub8 < 6, hi, jnp.where(sub8 == 6, 1.0, 0.0))
                lo = jnp.where(sub8 < 6, lo, 0.0)
                xb = jnp.concatenate([hi, lo], 0).astype(BF16)
                sel = jnp.broadcast_to(high[p : p + 1, :], (16, 128))
                left.append(
                    jnp.concatenate([jnp.where(sel == jnp.asarray(v, BF16), xb, jnp.zeros_like(xb)) for v in range(16)], 0)
                )
                right.append(jnp.where(digits == jnp.broadcast_to(low[p : p + 1, :], (256, 128)),
                                       jnp.ones((256, 128), BF16), jnp.zeros((256, 128), BF16)))
        acc[...] += nt(jnp.concatenate(left, 1), jnp.concatenate(right, 1))
        return carry

    lax.fori_loop(0, 128 // GRP_SRC, step, 0)

    lane = lanes((8, 128))

    def finish(s, carry):
        sel = s // 2
        old = jnp.zeros((8, 128), F32)
        for g in range(4):
            tile = recv[pl.ds(pl.multiple_of((s * 4 + g) * CH + 32, 8), 8), :]
            both = jnp.where(sub8 < 4, jnp.broadcast_to(tile[5:6, :], (8, 128)), jnp.broadcast_to(tile[6:7, :], (8, 128)))
            moved = jnp.zeros((8, 128), F32)
            for c in range(4):
                moved = jnp.where((sub8 & 3) == c, pltpu.roll(both, (32 * (g - c)) % 128, 1), moved)
            old = jnp.where((lane >> 5) == g, moved, old)
        old = jnp.where(sub8 < 6, old, 0.0)
        rows = acc[pl.ds(pl.multiple_of(sel * 16, 16), 16), :]
        rows = jnp.where((s & 1) == 0, rows[:, :128], rows[:, 128:])
        total = rows[0:8] + rows[8:16]
        count = jnp.broadcast_to(total[6:7, :], (8, 128))
        fresh = (total + PRIOR * old) / (count + PRIOR)
        out[s] = jnp.where(sub8 < 6, fresh, 0.0)
        return carry

    lax.fori_loop(0, 32, finish, 0, unroll=4)


def code_digits(x, first, second_cols, used):
    a = jnp.broadcast_to(x[6:7, :], (8, 128))
    b = jnp.broadcast_to(x[7:8, :], (8, 128))
    return a, b


def resid_part(place, recv, fresh, book, resid, table, left, acc):
    first = place[0]
    sub8 = subs((8, 128))
    lane = lanes((8, 128))
    digits = subs((256, 128)).astype(F32).astype(BF16)
    digit64 = subs((64, 128)).astype(F32).astype(BF16)
    for sel in range(16):
        for h in range(2):
            hi, lo = split(fresh[2 * sel + h])
            left[sel * 16 : (sel + 1) * 16, h * 128 : (h + 1) * 128] = jnp.concatenate([hi, lo], 0).astype(BF16)
    acc[...] = jnp.zeros((64, 128), F32)
    one, zero = jnp.ones((), BF16), jnp.zeros((), BF16)
    is_first = (sub8 < first) | (sub8 == 6)

    def step(i, carry):
        lhs, rhs = [], []
        for k in range(RES_SRC):
            src = i * RES_SRC + k
            base = pl.multiple_of(src * CH, 8)
            label, used = row_info(recv[pl.ds(base + 32, 8), :])
            low = (label & 255).astype(F32).astype(BF16)
            high = label >> 8
            hot = [jnp.where(digits == jnp.broadcast_to(low[p : p + 1, :], (256, 128)),
                             jnp.ones((256, 128), BF16), jnp.zeros((256, 128), BF16)) for p in range(4)]
            got = nn(left[...], jnp.concatenate(hot, 1))
            for p in range(4):
                x = recv[pl.ds(base + 8 * p, 8), :]
                sel = jnp.broadcast_to(high[p : p + 1, :], (8, 128))
                ghi = jnp.zeros((8, 128), F32)
                glo = jnp.zeros((8, 128), F32)
                for v in range(16):
                    hit = sel == v
                    ghi = jnp.where(hit, got[v * 16 : v * 16 + 8, p * 128 : (p + 1) * 128], ghi)
                    glo = jnp.where(hit, got[v * 16 + 8 : v * 16 + 16, p * 128 : (p + 1) * 128], glo)
                r = x - (ghi + glo)
                resid[src * 4 + p] = r
                a = jnp.broadcast_to(x[6:7, :], (8, 128))
                b = jnp.broadcast_to(x[7:8, :], (8, 128))
                code = jnp.where(is_first, a, b).astype(jnp.int32)
                use = used[p : p + 1, :]
                pick = jnp.where(jnp.broadcast_to(use, (8, 128)), code >> 6, -1).astype(F32)
                pick = jnp.concatenate([pick, pick], 0).astype(BF16)
                hi, lo = split(r)
                hi = jnp.where(sub8 < 6, hi, 1.0)
                lo = jnp.where(sub8 < 6, lo, 0.0)
                rb = jnp.concatenate([hi, lo], 0).astype(BF16)
                lhs.append(jnp.concatenate([jnp.where(pick == jnp.asarray(v, BF16), rb, jnp.zeros_like(rb)) for v in range(4)], 0))
                da = (x[6:7, :].astype(jnp.int32) & 63).astype(F32).astype(BF16)
                db = (x[7:8, :].astype(jnp.int32) & 63).astype(F32).astype(BF16)
                rhs.append(jnp.concatenate(
                    [jnp.where(digit64 == jnp.broadcast_to(d, (64, 128)), jnp.ones((64, 128), BF16), jnp.zeros((64, 128), BF16))
                     for d in (da, db)], 0))
        acc[...] += nt(jnp.concatenate(lhs, 1), jnp.concatenate(rhs, 1))
        return carry

    lax.fori_loop(0, 128 // RES_SRC, step, 0)

    valid = ((sub8 < first) == (lane < 64)) & (sub8 < 6)
    made = []
    for sel in range(4):
        total = acc[sel * 16 : sel * 16 + 8, :] + acc[sel * 16 + 8 : sel * 16 + 16, :]
        count = jnp.where(lane < 64, jnp.broadcast_to(total[6:7, :], (8, 128)), jnp.broadcast_to(total[7:8, :], (8, 128)))
        new = (total + PRIOR * book[sel]) / (count + PRIOR)
        new = jnp.where(valid, new, 0.0)
        table[sel] = new
        made.append(new + pltpu.roll(new, 64, 1))
    shown = [jnp.where(lane < 64, made[0], made[1]), jnp.where(lane < 64, made[2], made[3])]

    return shown


def error_part(place, recv, fresh, shown, resid, table, out, left, spread, mixed, stage, sems):
    first = place[0]
    sub8 = subs((8, 128))
    lane = lanes((8, 128))
    digit64 = subs((64, 128)).astype(F32).astype(BF16)
    is_first = sub8 < first
    for sel in range(4):
        hi, lo = split(table[sel])
        left[sel * 16 : (sel + 1) * 16, :] = jnp.concatenate([hi, lo], 0).astype(BF16)
    for g in range(4):
        for other in range(4):
            if other != g:
                spread[:, g * 64 : (g + 1) * 64, other * 128 : (other + 1) * 128] = jnp.zeros((16, 64, 128), BF16)

    def look(i, carry):
        hot, useds = [], []
        for k in range(8):
            src = i * 8 + k
            base = pl.multiple_of(src * CH, 8)
            unused, used = row_info(recv[pl.ds(base + 32, 8), :])
            useds.append(used)
            for p in range(4):
                r = resid[src * 4 + p]
                da = (r[6:7, :].astype(jnp.int32) & 63).astype(F32).astype(BF16)
                db = (r[7:8, :].astype(jnp.int32) & 63).astype(F32).astype(BF16)
                hot.append(jnp.concatenate(
                    [jnp.where(digit64 == jnp.broadcast_to(d, (64, 128)), jnp.ones((64, 128), BF16), jnp.zeros((64, 128), BF16))
                     for d in (da, db)], 0))
        got = nn(left[...], jnp.concatenate(hot, 1))
        errs = []
        for k in range(8):
            src = i * 8 + k
            for p in range(4):
                q = (k * 4 + p) * 128
                r = resid[src * 4 + p]
                a = jnp.broadcast_to(r[6:7, :], (8, 128))
                b = jnp.broadcast_to(r[7:8, :], (8, 128))
                pick = jnp.where(is_first, a, b).astype(jnp.int32) >> 6
                whi = jnp.zeros((8, 128), F32)
                wlo = jnp.zeros((8, 128), F32)
                for v in range(4):
                    hit = pick == v
                    whi = jnp.where(hit, got[v * 16 : v * 16 + 8, q : q + 128], whi)
                    wlo = jnp.where(hit, got[v * 16 + 8 : v * 16 + 16, q : q + 128], wlo)
                errs.append(jnp.where(jnp.broadcast_to(useds[k][p : p + 1, :], (8, 128)) & (sub8 < 6), r - (whi + wlo), 0.0))
        for g in range(4):
            rows = []
            for p in range(4):
                e0, e1 = errs[g * 4 + p], errs[(g + 4) * 4 + p]
                rows.append(jnp.where(lane < 64, e0, pltpu.roll(e1, 64, 1)))
                rows.append(jnp.where(lane < 64, pltpu.roll(e0, 64, 1), e1))
            spread[i, g * 64 : (g + 1) * 64, g * 128 : (g + 1) * 128] = jnp.concatenate(rows, 0).astype(BF16)
        return carry

    lax.fori_loop(0, 16, look, 0, unroll=2)

    spots = subs((256, 128)).astype(F32).astype(BF16)
    spot_lane = lanes((1, 128))

    def mix(sh, carry):
        total = jnp.zeros((512, 256), F32)
        hots, errs = [], []
        for pair in range(2):
            cols = []
            for g in range(4):
                aims = []
                for q in range(2):
                    src = sh * 16 + (2 * pair + q) * 4 + g
                    row = recv[pl.ds(src * CH + 36, 1), :].astype(jnp.int32)
                    aims.append((row >> 2) * 16 + (row & 3) + (2 * pair + q) * 4)
                aim = jnp.where(spot_lane < 64, aims[0], pltpu.roll(aims[1], 64, 1))
                halves = []
                for h in range(2):
                    at = jnp.broadcast_to((aim - 256 * h).astype(F32).astype(BF16), (256, 128))
                    halves.append(jnp.where(spots == at, jnp.ones((256, 128), BF16), jnp.zeros((256, 128), BF16)))
                cols.append(jnp.concatenate(halves, 0))
            hots.append(jnp.concatenate(cols, 1))
            errs.append(spread[sh * 2 + pair])
        got = nt(jnp.concatenate(hots, 1), jnp.concatenate(errs, 1))
        mixed[:, pl.ds(sh * 16, 16), :] = got.reshape(32, 16, 256)
        return carry

    lax.fori_loop(0, 8, mix, 0, unroll=2)

    def move(t):
        rows = pl.ds(pl.multiple_of(t * 4 * EC, 8), 4 * EC)
        return pltpu.make_async_copy(stage.at[rows], out.at[rows], sems.at[t])

    def finish(t, carry):
        for h in range(2):
            tile = mixed[t, :, h * 128 : (h + 1) * 128].T
            for g2 in range(2):
                base = pl.multiple_of((t * 4 + 2 * h + g2) * EC, 8)
                for r in range(8):
                    stage[pl.ds(base + r, 6, stride=8), :] = tile[g2 * 64 + r * 8 : g2 * 64 + r * 8 + 6, :]
                stage[pl.ds(base + 48, 8), :] = fresh[t]
                stage[pl.ds(base + 56, 8), :] = shown[0]
                stage[pl.ds(base + 64, 8), :] = shown[1]
        move(t).start()
        return carry

    lax.fori_loop(0, 32, finish, 0, unroll=8)

    def settle(t, carry):
        move(t).wait()
        return carry

    lax.fori_loop(0, 32, settle, 0)


def main_body(place, recv, book, out, sums, fresh, left, csum, resid, table, words, spread, mixed, stage, sems):
    sums_part(recv, fresh, sums)
    shown = resid_part(place, recv, fresh, book, resid, table, left, csum)
    error_part(place, recv, fresh, shown, resid, table, out, words, spread, mixed, stage, sems)


def place_body(landed, out, centroids, book, buf, extra, turned, cols, sems):
    moves = [
        pltpu.make_async_copy(landed.at[pl.ds(16 * k, 16), pl.ds(0, 48)], buf.at[pl.ds(16 * k, 16)], sems.at[k])
        for k in range(8)
    ]
    moves.append(pltpu.make_async_copy(landed.at[:, pl.ds(48, 24)], extra, sems.at[8]))
    for move in moves[8:] + moves[:8]:
        move.start()
    moves[8].wait()
    flat = extra.reshape(128 * 24, 128)
    for h in range(3):
        for c in range(6):
            cols[pl.ds(c, 128, stride=6), :] = flat[pl.ds(h * 8 + c, 128, stride=24), :]
        for w in range(6):
            tile = cols[w * 128 : (w + 1) * 128, :].T
            if h == 0:
                centroids[:, w * 128 : (w + 1) * 128] = tile
            else:
                book[(h - 1) * 128 : h * 128, w * 128 : (w + 1) * 128] = tile
    flat = buf.reshape(128 * 48, 128)
    ready = 0
    for w in range(6):
        need = (128 * w + 127) // 6 // 16 + 1
        for k in range(ready, need):
            moves[k].wait()
        ready = need
        for r in range(8):
            turned[w, pl.ds(r, 128, stride=8), :] = flat[pl.ds(w * 1024 + r, 128, stride=8), :].T
        out[:, :, w * 128 : (w + 1) * 128] = turned[w].reshape(128, 8, 128).astype(BF16)


def local(corpus, block_rows, targets, assign, codes, centroids, codebook):
    grp = lax.axis_index("grp")
    me = lax.axis_index("shard") * 4 + grp
    first = jnp.where(grp == 1, 2, jnp.where(grp == 2, 4, 6)).astype(jnp.int32)
    place = jnp.stack([first, grp])
    vmem, hbm, smem = (pl.BlockSpec(memory_space=m) for m in (pltpu.VMEM, pltpu.HBM, pltpu.SMEM))

    sent = call(
        send_body,
        [smem, hbm, hbm, hbm, vmem, vmem, vmem],
        vmem,
        jax.ShapeDtypeStruct((128 * CH, 128), F32),
        [
            pltpu.VMEM((768, 128), F32),
            pltpu.VMEM((128, 128), F32),
            pltpu.VMEM((128, 128), F32),
            pltpu.VMEM((512, 128), F32),
            pltpu.VMEM((6, 512, 128), F32),
            pltpu.VMEM((512, 96), jnp.int32),
            pltpu.VMEM((128, 768), F32),
            pltpu.SemaphoreType.DMA((8,)),
        ],
        SEND_MIB,
        moved=5 << 20,
    )(
        place,
        corpus.reshape(512, 768),
        codes.reshape(512, 96),
        centroids,
        targets.reshape(1, 64),
        block_rows.reshape(1, 64),
        assign.T,
    )
    recv = lax.all_to_all(sent.reshape(128, CH, 128), BOTH, 0, 0, tiled=True).reshape(128 * CH, 128)

    old = lax.dynamic_slice(codebook, (0, 6 * me), (256, 6)).T.reshape(6, 4, 64).transpose(1, 0, 2)
    old = jnp.pad(jnp.concatenate([old, old], 2), ((0, 0), (0, 2), (0, 0)))
    errors = call(
        main_body,
        [smem, vmem, vmem],
        hbm,
        jax.ShapeDtypeStruct((128 * EC, 128), F32),
        [
            pltpu.VMEM((256, 256), F32),
            pltpu.VMEM((32, 8, 128), F32),
            pltpu.VMEM((256, 256), BF16),
            pltpu.VMEM((64, 128), F32),
            pltpu.VMEM((512, 8, 128), F32),
            pltpu.VMEM((4, 8, 128), F32),
            pltpu.VMEM((64, 128), BF16),
            pltpu.VMEM((16, 256, 512), BF16),
            pltpu.VMEM((32, 128, 256), F32),
            pltpu.VMEM((128 * EC, 128), F32),
            pltpu.SemaphoreType.DMA((32,)),
        ],
        32,
        flops=1 << 34,
        moved=8 << 20,
    )(place, recv, old)
    landed = lax.all_to_all(errors.reshape(128, EC, 128), BOTH, 0, 0, tiled=True)

    moved_error, new_centroids, new_codebook = call(
        place_body,
        [hbm],
        (vmem, vmem, vmem),
        (
            jax.ShapeDtypeStruct((128, 8, 768), BF16),
            jax.ShapeDtypeStruct((128, 768), F32),
            jax.ShapeDtypeStruct((256, 768), F32),
        ),
        [
            pltpu.VMEM((128, 48, 128), F32),
            pltpu.VMEM((128, 24, 128), F32),
            pltpu.VMEM((6, 1024, 128), F32),
            pltpu.VMEM((768, 128), F32),
            pltpu.SemaphoreType.DMA((9,)),
        ],
        24,
        moved=7 << 20,
    )(landed)
    return (new_centroids, moved_error, new_codebook)


def solution(mesh):
    in_specs = (
        P(BOTH, None, None),
        P(BOTH),
        P(BOTH, None),
        P(BOTH, None),
        P(BOTH, None, None),
        P("shard", None),
        P(),
    )
    out_specs = (P("shard", None), P(BOTH, None, None), P())
    return jax.shard_map(local, mesh=mesh, in_specs=in_specs, out_specs=out_specs, check_vma=False)
```

```python
import jax
import jax.numpy as jnp
from jax import lax
from jax.experimental import pallas as pl
from jax.experimental.pallas import tpu as pltpu
from jax.sharding import PartitionSpec as P

PRIOR = 8.0
BOTH = ("shard", "grp")
F32 = jnp.float32
BF16 = jnp.bfloat16

CH = 40
EC = 72
FIRST = (0, 0, 1, 2)
SECOND = (0, 1, 2, 2)


def call(body, ins, outs, out, scratch, mib, flops=0, moved=0):
    return pl.pallas_call(
        body,
        in_specs=ins,
        out_specs=outs,
        out_shape=out,
        scratch_shapes=list(scratch),
        compiler_params=pltpu.CompilerParams(vmem_limit_bytes=mib << 20),
        cost_estimate=pl.CostEstimate(flops=flops, bytes_accessed=moved, transcendentals=0),
    )


def nt(a, b):
    return lax.dot_general(a, b, (((1,), (1,)), ((), ())), preferred_element_type=F32)


def nn(a, b):
    return lax.dot_general(a, b, (((1,), (0,)), ((), ())), preferred_element_type=F32)


def lanes(shape):
    return lax.broadcasted_iota(jnp.int32, shape, len(shape) - 1)


def subs(shape):
    return lax.broadcasted_iota(jnp.int32, shape, len(shape) - 2)


def split(x):
    hi = x.astype(BF16).astype(F32)
    return hi, x - hi


def send_body(place, corpus, codes, cent, dest, counts, assign, sent, turned, words, rows_s, codes_s, rows_c, codes_i, cent_s, stage, sems):
    out = stage.reshape(128 * CH, 128)
    leave = [pltpu.make_async_copy(stage.at[:, pl.ds(8 * p, 8)], sent.at[:, pl.ds(8 * p, 8)], sems.at[8 + p]) for p in range(5)]
    moves = [pltpu.make_async_copy(corpus.at[:, pl.ds(w * 128, 128)], rows_c.at[w], sems.at[w]) for w in range(6)]
    moves.append(pltpu.make_async_copy(codes, codes_i, sems.at[6]))
    moves.append(pltpu.make_async_copy(cent, cent_s, sems.at[7]))
    for move in moves:
        move.start()
    lane = lanes((1, 128))
    here = dest[...].astype(F32)
    here = jnp.broadcast_to(jnp.concatenate([here, here], 1), (128, 128))
    there = here.T
    before = (there == here) & (subs((128, 128)) < lanes((128, 128)))
    rank = jnp.sum(jnp.where(before, 1.0, 0.0), axis=0, keepdims=True)
    slot = here[0:1, :] * 4.0 + rank
    used = counts[...].astype(F32)
    used = jnp.concatenate([used, used], 1)
    labels = assign[...].astype(F32)
    labels = jnp.concatenate([labels, labels], 1)
    infos = [jnp.where(lane < 64, labels[2 * p : 2 * p + 1, :], labels[2 * p + 1 : 2 * p + 2, :]) for p in range(4)]
    infos.append(jnp.where(lane < 64, slot, used))
    for k in range(5):
        out[pl.ds(32 + k, 128, stride=CH), :] = jnp.broadcast_to(infos[k], (128, 128))
    out[pl.ds(39, 128, stride=CH), :] = jnp.zeros((128, 128), F32)
    moves[6].wait()
    codes_s[:, 0:96] = codes_i[...].astype(F32)
    codes_s[:, 96:128] = jnp.zeros((512, 32), F32)
    moves[7].wait()
    start = pl.multiple_of(place[1] * 32, 32)
    for w in range(6):
        rows_s[0:32, :] = cent_s[pl.ds(start, 32), w * 128 : (w + 1) * 128]
        rows_s[32:128, :] = jnp.zeros((96, 128), F32)
        turned[w * 128 : (w + 1) * 128, :] = rows_s[...].T
    parts = [turned[pl.ds(c, 128, stride=6), :] for c in range(6)]
    for k, cols in ((5, (0, 1, 2, 3)), (6, (4, 5))):
        row = parts[cols[0]]
        for i, c in enumerate(cols[1:], 1):
            row = row + pltpu.roll(parts[c], 32 * i, 1)
        out[pl.ds(32 + k, 128, stride=CH), :] = row
    leave[4].start()
    for p in range(4):
        for h in range(2):
            rows_s[h * 64 : (h + 1) * 64, :] = codes_s[pl.ds(2 * p + h, 64, stride=8), :]
        words[...] = rows_s[...].T
        for j in range(4):
            for k, pick in ((6, FIRST[j]), (7, SECOND[j])):
                out[pl.ds(j * CH + p * 8 + k, 32, stride=4 * CH), :] = words[pl.ds(pick, 32, stride=3), :]
        for w in range(6):
            if p == 0:
                moves[w].wait()
            for h in range(2):
                rows_s[h * 64 : (h + 1) * 64, :] = rows_c[w, pl.ds(2 * p + h, 64, stride=8), :]
            turned[w * 128 : (w + 1) * 128, :] = rows_s[...].T
        for c in range(6):
            out[pl.ds(p * 8 + c, 128, stride=CH), :] = turned[pl.ds(c, 128, stride=6), :]
        leave[p].start()
    for copy in leave:
        copy.wait()


def row_info(tile):
    lane = lanes((8, 128))
    counts = tile[4:5, :]
    counts = jnp.where(lane[0:1] < 64, pltpu.roll(counts, 64, 1), counts)
    place = 2 * subs((8, 128)) + (lane >= 64).astype(jnp.int32)
    used = place < counts.astype(jnp.int32)
    return tile.astype(jnp.int32), used


GRP_SRC = 32
RES_SRC = 32
SEND_MIB = 56
LOOK_SRC = 8


def sums_part(recv, out, acc):
    acc[...] = jnp.zeros((256, 256), F32)
    sub8 = subs((8, 128))
    digits = subs((256, 128)).astype(F32).astype(BF16)

    def step(i, carry):
        left, right = [], []
        for k in range(GRP_SRC):
            base = pl.multiple_of((i * GRP_SRC + k) * CH, 8)
            label, used = row_info(recv[pl.ds(base + 32, 8), :])
            low = jnp.where(used, label & 255, -1).astype(F32).astype(BF16)
            high = (label >> 8).astype(F32).astype(BF16)
            for p in range(4):
                x = recv[pl.ds(base + 8 * p, 8), :]
                hi, lo = split(x)
                hi = jnp.where(sub8 < 6, hi, jnp.where(sub8 == 6, 1.0, 0.0))
                lo = jnp.where(sub8 < 6, lo, 0.0)
                xb = jnp.concatenate([hi, lo], 0).astype(BF16)
                sel = jnp.broadcast_to(high[p : p + 1, :], (16, 128))
                left.append(
                    jnp.concatenate([jnp.where(sel == jnp.asarray(v, BF16), xb, jnp.zeros_like(xb)) for v in range(16)], 0)
                )
                right.append(jnp.where(digits == jnp.broadcast_to(low[p : p + 1, :], (256, 128)),
                                       jnp.ones((256, 128), BF16), jnp.zeros((256, 128), BF16)))
        acc[...] += nt(jnp.concatenate(left, 1), jnp.concatenate(right, 1))
        return carry

    lax.fori_loop(0, 128 // GRP_SRC, step, 0)

    lane = lanes((8, 128))

    def finish(s, carry):
        sel = s // 2
        old = jnp.zeros((8, 128), F32)
        for g in range(4):
            tile = recv[pl.ds(pl.multiple_of((s * 4 + g) * CH + 32, 8), 8), :]
            both = jnp.where(sub8 < 4, jnp.broadcast_to(tile[5:6, :], (8, 128)), jnp.broadcast_to(tile[6:7, :], (8, 128)))
            moved = jnp.zeros((8, 128), F32)
            for c in range(4):
                moved = jnp.where((sub8 & 3) == c, pltpu.roll(both, (32 * (g - c)) % 128, 1), moved)
            old = jnp.where((lane >> 5) == g, moved, old)
        old = jnp.where(sub8 < 6, old, 0.0)
        rows = acc[pl.ds(pl.multiple_of(sel * 16, 16), 16), :]
        rows = jnp.where((s & 1) == 0, rows[:, :128], rows[:, 128:])
        total = rows[0:8] + rows[8:16]
        count = jnp.broadcast_to(total[6:7, :], (8, 128))
        fresh = (total + PRIOR * old) / (count + PRIOR)
        out[s] = jnp.where(sub8 < 6, fresh, 0.0)
        return carry

    lax.fori_loop(0, 32, finish, 0, unroll=4)


def code_digits(x, first, second_cols, used):
    a = jnp.broadcast_to(x[6:7, :], (8, 128))
    b = jnp.broadcast_to(x[7:8, :], (8, 128))
    return a, b


def resid_part(place, recv, fresh, book, resid, table, left, acc):
    first = place[0]
    sub8 = subs((8, 128))
    lane = lanes((8, 128))
    digits = subs((256, 128)).astype(F32).astype(BF16)
    digit64 = subs((64, 128)).astype(F32).astype(BF16)
    for sel in range(16):
        for h in range(2):
            hi, lo = split(fresh[2 * sel + h])
            left[sel * 16 : (sel + 1) * 16, h * 128 : (h + 1) * 128] = jnp.concatenate([hi, lo], 0).astype(BF16)
    acc[...] = jnp.zeros((64, 128), F32)
    one, zero = jnp.ones((), BF16), jnp.zeros((), BF16)
    is_first = (sub8 < first) | (sub8 == 6)

    def step(i, carry):
        lhs, rhs = [], []
        for k in range(RES_SRC):
            src = i * RES_SRC + k
            base = pl.multiple_of(src * CH, 8)
            label, used = row_info(recv[pl.ds(base + 32, 8), :])
            low = (label & 255).astype(F32).astype(BF16)
            high = label >> 8
            hot = [jnp.where(digits == jnp.broadcast_to(low[p : p + 1, :], (256, 128)),
                             jnp.ones((256, 128), BF16), jnp.zeros((256, 128), BF16)) for p in range(4)]
            got = nn(left[...], jnp.concatenate(hot, 1))
            for p in range(4):
                x = recv[pl.ds(base + 8 * p, 8), :]
                sel = jnp.broadcast_to(high[p : p + 1, :], (8, 128))
                ghi = jnp.zeros((8, 128), F32)
                glo = jnp.zeros((8, 128), F32)
                for v in range(16):
                    hit = sel == v
                    ghi = jnp.where(hit, got[v * 16 : v * 16 + 8, p * 128 : (p + 1) * 128], ghi)
                    glo = jnp.where(hit, got[v * 16 + 8 : v * 16 + 16, p * 128 : (p + 1) * 128], glo)
                r = x - (ghi + glo)
                resid[src * 4 + p] = r
                a = jnp.broadcast_to(x[6:7, :], (8, 128))
                b = jnp.broadcast_to(x[7:8, :], (8, 128))
                code = jnp.where(is_first, a, b).astype(jnp.int32)
                use = used[p : p + 1, :]
                pick = jnp.where(jnp.broadcast_to(use, (8, 128)), code >> 6, -1).astype(F32)
                pick = jnp.concatenate([pick, pick], 0).astype(BF16)
                hi, lo = split(r)
                hi = jnp.where(sub8 < 6, hi, 1.0)
                lo = jnp.where(sub8 < 6, lo, 0.0)
                rb = jnp.concatenate([hi, lo], 0).astype(BF16)
                lhs.append(jnp.concatenate([jnp.where(pick == jnp.asarray(v, BF16), rb, jnp.zeros_like(rb)) for v in range(4)], 0))
                da = (x[6:7, :].astype(jnp.int32) & 63).astype(F32).astype(BF16)
                db = (x[7:8, :].astype(jnp.int32) & 63).astype(F32).astype(BF16)
                rhs.append(jnp.concatenate(
                    [jnp.where(digit64 == jnp.broadcast_to(d, (64, 128)), jnp.ones((64, 128), BF16), jnp.zeros((64, 128), BF16))
                     for d in (da, db)], 0))
        acc[...] += nt(jnp.concatenate(lhs, 1), jnp.concatenate(rhs, 1))
        return carry

    lax.fori_loop(0, 128 // RES_SRC, step, 0)

    valid = ((sub8 < first) == (lane < 64)) & (sub8 < 6)
    made = []
    for sel in range(4):
        total = acc[sel * 16 : sel * 16 + 8, :] + acc[sel * 16 + 8 : sel * 16 + 16, :]
        count = jnp.where(lane < 64, jnp.broadcast_to(total[6:7, :], (8, 128)), jnp.broadcast_to(total[7:8, :], (8, 128)))
        new = (total + PRIOR * book[sel]) / (count + PRIOR)
        new = jnp.where(valid, new, 0.0)
        table[sel] = new
        made.append(new + pltpu.roll(new, 64, 1))
    shown = [jnp.where(lane < 64, made[0], made[1]), jnp.where(lane < 64, made[2], made[3])]

    return shown


def error_part(place, recv, fresh, shown, resid, table, out, left, spread, mixed, stage, sems):
    first = place[0]
    sub8 = subs((8, 128))
    lane = lanes((8, 128))
    digit64 = subs((64, 128)).astype(F32).astype(BF16)
    is_first = sub8 < first
    for sel in range(4):
        hi, lo = split(table[sel])
        left[sel * 16 : (sel + 1) * 16, :] = jnp.concatenate([hi, lo], 0).astype(BF16)
    for g in range(4):
        for other in range(4):
            if other != g:
                spread[:, g * 64 : (g + 1) * 64, other * 128 : (other + 1) * 128] = jnp.zeros((16, 64, 128), BF16)

    def look(i, carry):
        hot, useds = [], []
        for k in range(8):
            src = i * 8 + k
            base = pl.multiple_of(src * CH, 8)
            unused, used = row_info(recv[pl.ds(base + 32, 8), :])
            useds.append(used)
            for p in range(4):
                r = resid[src * 4 + p]
                da = (r[6:7, :].astype(jnp.int32) & 63).astype(F32).astype(BF16)
                db = (r[7:8, :].astype(jnp.int32) & 63).astype(F32).astype(BF16)
                hot.append(jnp.concatenate(
                    [jnp.where(digit64 == jnp.broadcast_to(d, (64, 128)), jnp.ones((64, 128), BF16), jnp.zeros((64, 128), BF16))
                     for d in (da, db)], 0))
        got = nn(left[...], jnp.concatenate(hot, 1))
        errs = []
        for k in range(8):
            src = i * 8 + k
            for p in range(4):
                q = (k * 4 + p) * 128
                r = resid[src * 4 + p]
                a = jnp.broadcast_to(r[6:7, :], (8, 128))
                b = jnp.broadcast_to(r[7:8, :], (8, 128))
                pick = jnp.where(is_first, a, b).astype(jnp.int32) >> 6
                whi = jnp.zeros((8, 128), F32)
                wlo = jnp.zeros((8, 128), F32)
                for v in range(4):
                    hit = pick == v
                    whi = jnp.where(hit, got[v * 16 : v * 16 + 8, q : q + 128], whi)
                    wlo = jnp.where(hit, got[v * 16 + 8 : v * 16 + 16, q : q + 128], wlo)
                errs.append(jnp.where(jnp.broadcast_to(useds[k][p : p + 1, :], (8, 128)) & (sub8 < 6), r - (whi + wlo), 0.0))
        for g in range(4):
            rows = []
            for p in range(4):
                e0, e1 = errs[g * 4 + p], errs[(g + 4) * 4 + p]
                rows.append(jnp.where(lane < 64, e0, pltpu.roll(e1, 64, 1)))
                rows.append(jnp.where(lane < 64, pltpu.roll(e0, 64, 1), e1))
            spread[i, g * 64 : (g + 1) * 64, g * 128 : (g + 1) * 128] = jnp.concatenate(rows, 0).astype(BF16)
        return carry

    lax.fori_loop(0, 16, look, 0, unroll=4)

    spots = subs((256, 128)).astype(F32).astype(BF16)
    spot_lane = lanes((1, 128))

    def mix(sh, carry):
        total = jnp.zeros((512, 256), F32)
        hots, errs = [], []
        for pair in range(2):
            cols = []
            for g in range(4):
                aims = []
                for q in range(2):
                    src = sh * 16 + (2 * pair + q) * 4 + g
                    row = recv[pl.ds(src * CH + 36, 1), :].astype(jnp.int32)
                    aims.append((row >> 2) * 16 + (row & 3) + (2 * pair + q) * 4)
                aim = jnp.where(spot_lane < 64, aims[0], pltpu.roll(aims[1], 64, 1))
                halves = []
                for h in range(2):
                    at = jnp.broadcast_to((aim - 256 * h).astype(F32).astype(BF16), (256, 128))
                    halves.append(jnp.where(spots == at, jnp.ones((256, 128), BF16), jnp.zeros((256, 128), BF16)))
                cols.append(jnp.concatenate(halves, 0))
            hots.append(jnp.concatenate(cols, 1))
            errs.append(spread[sh * 2 + pair])
        got = nt(jnp.concatenate(hots, 1), jnp.concatenate(errs, 1))
        mixed[:, pl.ds(sh * 16, 16), :] = got.reshape(32, 16, 256)
        return carry

    lax.fori_loop(0, 8, mix, 0, unroll=4)

    def move(t):
        rows = pl.ds(pl.multiple_of(t * 4 * EC, 8), 4 * EC)
        return pltpu.make_async_copy(stage.at[rows], out.at[rows], sems.at[t])

    def finish(t, carry):
        for h in range(2):
            tile = mixed[t, :, h * 128 : (h + 1) * 128].T
            for g2 in range(2):
                base = pl.multiple_of((t * 4 + 2 * h + g2) * EC, 8)
                for r in range(8):
                    stage[pl.ds(base + r, 6, stride=8), :] = tile[g2 * 64 + r * 8 : g2 * 64 + r * 8 + 6, :]
                stage[pl.ds(base + 48, 8), :] = fresh[t]
                stage[pl.ds(base + 56, 8), :] = shown[0]
                stage[pl.ds(base + 64, 8), :] = shown[1]
        move(t).start()
        return carry

    lax.fori_loop(0, 32, finish, 0, unroll=8)

    def settle(t, carry):
        move(t).wait()
        return carry

    lax.fori_loop(0, 32, settle, 0)


def main_body(place, recv, book, out, sums, fresh, left, csum, resid, table, words, spread, mixed, stage, sems):
    sums_part(recv, fresh, sums)
    shown = resid_part(place, recv, fresh, book, resid, table, left, csum)
    error_part(place, recv, fresh, shown, resid, table, out, words, spread, mixed, stage, sems)


def place_body(landed, out, centroids, book, buf, extra, turned, cols, sems):
    moves = [
        pltpu.make_async_copy(landed.at[pl.ds(16 * k, 16), pl.ds(0, 48)], buf.at[pl.ds(16 * k, 16)], sems.at[k])
        for k in range(8)
    ]
    moves.append(pltpu.make_async_copy(landed.at[:, pl.ds(48, 24)], extra, sems.at[8]))
    for move in moves[8:] + moves[:8]:
        move.start()
    moves[8].wait()
    flat = extra.reshape(128 * 24, 128)
    for h in range(3):
        for c in range(6):
            cols[pl.ds(c, 128, stride=6), :] = flat[pl.ds(h * 8 + c, 128, stride=24), :]
        for w in range(6):
            tile = cols[w * 128 : (w + 1) * 128, :].T
            if h == 0:
                centroids[:, w * 128 : (w + 1) * 128] = tile
            else:
                book[(h - 1) * 128 : h * 128, w * 128 : (w + 1) * 128] = tile
    flat = buf.reshape(128 * 48, 128)
    ready = 0
    for w in range(6):
        need = (128 * w + 127) // 6 // 16 + 1
        for k in range(ready, need):
            moves[k].wait()
        ready = need
        for r in range(8):
            turned[w, pl.ds(r, 128, stride=8), :] = flat[pl.ds(w * 1024 + r, 128, stride=8), :].T
        out[:, :, w * 128 : (w + 1) * 128] = turned[w].reshape(128, 8, 128).astype(BF16)


def local(corpus, block_rows, targets, assign, codes, centroids, codebook):
    grp = lax.axis_index("grp")
    me = lax.axis_index("shard") * 4 + grp
    first = jnp.where(grp == 1, 2, jnp.where(grp == 2, 4, 6)).astype(jnp.int32)
    place = jnp.stack([first, grp])
    vmem, hbm, smem = (pl.BlockSpec(memory_space=m) for m in (pltpu.VMEM, pltpu.HBM, pltpu.SMEM))

    sent = call(
        send_body,
        [smem, hbm, hbm, hbm, vmem, vmem, vmem],
        hbm,
        jax.ShapeDtypeStruct((128, CH, 128), F32),
        [
            pltpu.VMEM((768, 128), F32),
            pltpu.VMEM((128, 128), F32),
            pltpu.VMEM((128, 128), F32),
            pltpu.VMEM((512, 128), F32),
            pltpu.VMEM((6, 512, 128), F32),
            pltpu.VMEM((512, 96), jnp.int32),
            pltpu.VMEM((128, 768), F32),
            pltpu.VMEM((128, CH, 128), F32),
            pltpu.SemaphoreType.DMA((13,)),
        ],
        SEND_MIB,
        moved=5 << 20,
    )(
        place,
        corpus.reshape(512, 768),
        codes.reshape(512, 96),
        centroids,
        targets.reshape(1, 64),
        block_rows.reshape(1, 64),
        assign.T,
    )
    recv = lax.all_to_all(sent, BOTH, 0, 0, tiled=True).reshape(128 * CH, 128)

    old = lax.dynamic_slice(codebook, (0, 6 * me), (256, 6)).T.reshape(6, 4, 64).transpose(1, 0, 2)
    old = jnp.pad(jnp.concatenate([old, old], 2), ((0, 0), (0, 2), (0, 0)))
    errors = call(
        main_body,
        [smem, vmem, vmem],
        hbm,
        jax.ShapeDtypeStruct((128 * EC, 128), F32),
        [
            pltpu.VMEM((256, 256), F32),
            pltpu.VMEM((32, 8, 128), F32),
            pltpu.VMEM((256, 256), BF16),
            pltpu.VMEM((64, 128), F32),
            pltpu.VMEM((512, 8, 128), F32),
            pltpu.VMEM((4, 8, 128), F32),
            pltpu.VMEM((64, 128), BF16),
            pltpu.VMEM((16, 256, 512), BF16),
            pltpu.VMEM((32, 128, 256), F32),
            pltpu.VMEM((128 * EC, 128), F32),
            pltpu.SemaphoreType.DMA((32,)),
        ],
        32,
        flops=1 << 34,
        moved=8 << 20,
    )(place, recv, old)
    landed = lax.all_to_all(errors.reshape(128, EC, 128), BOTH, 0, 0, tiled=True)

    moved_error, new_centroids, new_codebook = call(
        place_body,
        [hbm],
        (vmem, vmem, vmem),
        (
            jax.ShapeDtypeStruct((128, 8, 768), BF16),
            jax.ShapeDtypeStruct((128, 768), F32),
            jax.ShapeDtypeStruct((256, 768), F32),
        ),
        [
            pltpu.VMEM((128, 48, 128), F32),
            pltpu.VMEM((128, 24, 128), F32),
            pltpu.VMEM((6, 1024, 128), F32),
            pltpu.VMEM((768, 128), F32),
            pltpu.SemaphoreType.DMA((9,)),
        ],
        24,
        moved=7 << 20,
    )(landed)
    return (new_centroids, moved_error, new_codebook)


def solution(mesh):
    in_specs = (
        P(BOTH, None, None),
        P(BOTH),
        P(BOTH, None),
        P(BOTH, None),
        P(BOTH, None, None),
        P("shard", None),
        P(),
    )
    out_specs = (P("shard", None), P(BOTH, None, None), P())
    return jax.shard_map(local, mesh=mesh, in_specs=in_specs, out_specs=out_specs, check_vma=False)
```
